128 devices in a mesh: tm: 64 (over z, y_hi, x, core), segment: 2 (over y_lo).
Axes of the slice: x: 4, y: 4 (y_hi: 2, y_lo: 2; y = y_hi * 2 + y_lo), z: 4, core: 2. Of those that a mesh axis runs over, the one named last changes fastest.
Arguments:
- tokens: bfloat16 [16384, 2560], P('tm'), may hold values from -6 to 6
- probes: int32 [2, 16384, 2560], P(None, 'tm'), may hold values from -1 to 1, as said below
- norm_gain: float32 [2560], replicated, may hold values from 0.1 to 1.9
- w_query: bfloat16 [2560, 2560], P('tm', 'segment'), may hold values from -0.125 to 0.125
- w_key: bfloat16 [2560, 2560], P('tm', 'segment'), may hold values from -0.125 to 0.125
- w_value: bfloat16 [2560, 2560], P('tm', 'segment'), may hold values from -0.125 to 0.125
- query_gain: float32 [2560], P('segment'), may hold values from 0.1 to 1.9
- key_gain: float32 [2560], P('segment'), may hold values from 0.1 to 1.9
- w_out: bfloat16 [2560, 2560], P('tm', 'segment'), may hold values from -0.125 to 0.125
Outputs:
- velocity: bfloat16 [16384, 2560], P('tm', 'segment')
- density: float32 [16384], P('tm')
The draws below stay inside these ranges and needn't reach their ends.
Inputs may be any that keep to these rules, and one draw needn't show every extreme that they name: `probes`: each entry is -1 or 1.
All inputs are finite; a program needn't handle non-finite values.
Results may differ from the reference program's by a relative error of at most 0.013.
Values may be sent and summed in bfloat16 or wider, within the bound.
A program may use at most 128 MiB of HBM per device.

```python
import math
import jax
import jax.numpy as jnp
from jax import lax

D = 2560
HEADS = 20
HEAD_DIM = 128
PROBES = 2
TOK_DEV = 256
WIN = 128
TOKENS = 16384
N_TM = 64


def draw_probes(key, part):
    key = jax.random.fold_in(key, 7)
    signs = jax.random.randint(key, (PROBES, TOKENS, D), 0, 2, dtype=jnp.int32)
    return (2 * signs - 1).astype(jnp.int32)


def level_of(stream_key, dims, pieces, smallest, top_value):
    loudness, own = 1.0, jax.random.fold_in(stream_key, 6)
    for dim, blocks in pieces:
        steps = jnp.exp(jax.random.uniform(jax.random.fold_in(own, dim), (blocks,), jnp.float32, smallest / len(pieces), top_value / len(pieces)))
        loudness = loudness * jnp.repeat(steps, dims[dim] // blocks).reshape([-1 if axis == dim else 1 for axis in range(len(dims))])
    return loudness


def centred(key, shape, scale, limit, pieces=(), kind=jnp.bfloat16):
    level = level_of(key, shape, pieces, -0.22, 0.18) if pieces else 1.0
    values = jax.random.normal(key, shape, jnp.float32) * scale * level
    return jnp.minimum(jnp.maximum(values, -limit), limit).astype(kind)


def setup_inputs(seed: int = 0) -> dict:
    key_list = jax.random.split(jax.random.key(seed), 10)
    return {
        "tokens": centred(key_list[0], (TOKENS, D), 1.0, 6.0, ((0, 64),)),
        "probes": draw_probes(jax.random.fold_in(key_list[9], 71), 0),
        "norm_gain": jnp.clip(1.0 + 0.18 * jax.random.normal(key_list[2], (D,), jnp.float32), 0.1, 1.9),
        "w_query": centred(key_list[3], (D, HEADS * HEAD_DIM), D ** -0.5, 0.125, ((0, 64), (1, 2))),
        "w_key": centred(key_list[4], (D, HEADS * HEAD_DIM), D ** -0.5, 0.125, ((0, 64), (1, 2))),
        "w_value": centred(key_list[5], (D, HEADS * HEAD_DIM), D ** -0.5, 0.125, ((0, 64), (1, 2))),
        "query_gain": jnp.clip(1.0 + 0.18 * jax.random.normal(key_list[6], (HEADS * HEAD_DIM,), jnp.float32), 0.1, 1.9),
        "key_gain": jnp.clip(1.0 + 0.18 * jax.random.normal(key_list[7], (HEADS * HEAD_DIM,), jnp.float32), 0.1, 1.9),
        "w_out": centred(key_list[8], (D, HEADS * HEAD_DIM), (HEADS * HEAD_DIM) ** -0.5, 0.125, ((0, 64), (1, 2))),
    }


eps = 1e-06

def norm_pair(value, tangent, gain):
    square = lax.optimization_barrier(jnp.mean(value * value, axis=-1, keepdims=True)) + eps
    factor = lax.rsqrt(square)
    inner = lax.optimization_barrier(jnp.mean(value * tangent, axis=-1, keepdims=True))
    return (value * factor * gain, (tangent * factor - value * (factor * factor * factor) * inner) * gain)

def window_mask(query_place, key_place, total):
    offset = query_place[:, None] - key_place[None, :]
    inside = (key_place[None, :] >= 0) & (key_place[None, :] < total)
    return (offset <= WIN) & (offset >= -WIN) & inside

def attend(query, query_tan, keys, keys_tan, values, values_tan, valid):
    scale = 1.0 / math.sqrt(query.shape[-1])
    query32 = query.astype(jnp.float32)
    query_tan32 = query_tan.astype(jnp.float32)
    keys32 = keys.astype(jnp.float32)
    keys_tan32 = keys_tan.astype(jnp.float32)
    values32 = values.astype(jnp.float32)
    values_tan32 = values_tan.astype(jnp.float32)
    scores = jnp.einsum('qhd,khd->hqk', query32, keys32) * scale
    weights = jnp.where(valid, jnp.exp(scores), 0.0)
    weights = weights / lax.optimization_barrier(jnp.sum(weights, axis=-1, keepdims=True))
    scores_tan = (jnp.einsum('pqhd,khd->phqk', query_tan32, keys32) + jnp.einsum('qhd,pkhd->phqk', query32, keys_tan32)) * scale
    scores_tan = jnp.where(valid, scores_tan, 0.0)
    weights_tan = weights * (scores_tan - lax.optimization_barrier(jnp.sum(weights * scores_tan, axis=-1, keepdims=True)))
    weights_low = weights.astype(jnp.bfloat16).astype(jnp.float32)
    weights_tan_low = weights_tan.astype(jnp.bfloat16).astype(jnp.float32)
    output = jnp.einsum('hqk,khd->qhd', weights_low, values32)
    output_tan = jnp.einsum('phqk,khd->pqhd', weights_tan_low, values32) + jnp.einsum('hqk,pkhd->pqhd', weights_low, values_tan32)
    return (output.astype(jnp.bfloat16), output_tan.astype(jnp.bfloat16))

def reference(tokens, probes, norm_gain, w_query, w_key, w_value, query_gain, key_gain, w_out):
    value = tokens.astype(jnp.float32)
    tangent = probes.astype(jnp.float32)
    normed, normed_tan = norm_pair(value, tangent, norm_gain)
    rows_all = jnp.concatenate([normed[None], normed_tan], 0).astype(jnp.bfloat16).reshape((PROBES + 1) * TOKENS, D)

    def project(weight):
        return jnp.dot(rows_all, weight, preferred_element_type=jnp.float32).reshape(PROBES + 1, TOKENS, HEADS, HEAD_DIM)

    def norm_heads(full, gain):
        normal, normal_tan = norm_pair(full[0], full[1:], gain.reshape(HEADS, HEAD_DIM))
        return (normal.astype(jnp.bfloat16), normal_tan.astype(jnp.bfloat16))
    query, query_tan = norm_heads(project(w_query), query_gain)
    keys, keys_tan = norm_heads(project(w_key), key_gain)
    value_all = project(w_value).astype(jnp.bfloat16)
    values, values_tan = (value_all[0], value_all[1:])
    keys_pad = jnp.pad(keys, ((WIN, WIN), (0, 0), (0, 0)))
    values_pad = jnp.pad(values, ((WIN, WIN), (0, 0), (0, 0)))
    keys_tan_pad = jnp.pad(keys_tan, ((0, 0), (WIN, WIN), (0, 0), (0, 0)))
    values_tan_pad = jnp.pad(values_tan, ((0, 0), (WIN, WIN), (0, 0), (0, 0)))
    span = TOK_DEV + 2 * WIN

    def block(index):
        start = index * TOK_DEV
        block_query = lax.dynamic_slice_in_dim(query, start, TOK_DEV, 0)
        block_query_tan = lax.dynamic_slice_in_dim(query_tan, start, TOK_DEV, 1)
        block_keys = lax.dynamic_slice_in_dim(keys_pad, start, span, 0)
        block_values = lax.dynamic_slice_in_dim(values_pad, start, span, 0)
        block_keys_tan = lax.dynamic_slice_in_dim(keys_tan_pad, start, span, 1)
        block_values_tan = lax.dynamic_slice_in_dim(values_tan_pad, start, span, 1)
        query_place = start + jnp.arange(TOK_DEV, dtype=jnp.int32)
        key_place = start - WIN + jnp.arange(span, dtype=jnp.int32)
        valid = window_mask(query_place, key_place, TOKENS)
        return attend(block_query, block_query_tan, block_keys, block_keys_tan, block_values, block_values_tan, valid)
    output, output_tan = lax.map(block, jnp.arange(N_TM, dtype=jnp.int32))
    output = output.reshape(1, TOKENS, HEADS * HEAD_DIM)
    output_tan = jnp.transpose(output_tan, (1, 0, 2, 3, 4)).reshape(PROBES, TOKENS, HEADS * HEAD_DIM)
    out_rows = jnp.concatenate([output, output_tan], 0).reshape((PROBES + 1) * TOKENS, HEADS * HEAD_DIM)
    terms = lax.dot_general(out_rows, w_out, (((1,), (1,)), ((), ())), preferred_element_type=jnp.float32)
    velocity = terms[:TOKENS].astype(jnp.bfloat16)
    terms_tan = terms[TOKENS:].reshape(PROBES, TOKENS, D)
    density = lax.optimization_barrier(jnp.sum(tangent * terms_tan, axis=(0, 2))) / (PROBES * math.sqrt(D))
    return (velocity, density)
```

```python
import math

import jax
import jax.numpy as jnp
from jax import lax
from jax.experimental import pallas as pl
from jax.experimental.pallas import tpu as pltpu
from jax.sharding import PartitionSpec as P

HEAD_DIM = 128
WIN = 128


eps = 1e-06
MESH = pl.DeviceIdType.MESH
R = 80

def gather_kernel(wk, wv, wq, wo, W, own, stage, got, local_sem, stage_sem, send_sem, recv_sem):
    me = lax.axis_index("tm")
    core = lax.rem(me, 2)
    x = lax.rem(me // 2, 4)
    yh = lax.rem(me // 8, 2)
    z = me // 16
    flip = core == 0
    a = jnp.where(flip, x, z); b = jnp.where(flip, z, x)
    sa = jnp.where(flip, 2, 16); sb = jnp.where(flip, 16, 2)
    ra = jnp.where(flip, 1, 8); rb = jnp.where(flip, 8, 1)
    def ring(p, d): return lax.rem(p + d + 4, 4)
    dev_a = [me + (ring(a, 1) - a) * sa, me + (ring(a, -1) - a) * sa]
    dev_b = [me + (ring(b, 1) - b) * sb, me + (ring(b, -1) - b) * sb]
    sib = me + 1 - 2 * core
    dev_y = me + (1 - 2 * yh) * 8
    barrier = pltpu.get_barrier_semaphore()
    peers = [sib, dev_y, *dev_a, *dev_b]
    for d in peers:
        pl.semaphore_signal(barrier, inc=1, device_id={"tm": d}, device_id_type=MESH)
    f = jnp.float32
    mine0 = jnp.where(flip, wk[...].astype(f), wv[...].astype(f))
    mine1 = jnp.where(flip, wq[...].astype(f), wo[...].astype(f))
    theirs0 = jnp.where(flip, wv[...].astype(f), wk[...].astype(f))
    theirs1 = jnp.where(flip, wo[...].astype(f), wq[...].astype(f))
    stage[...] = jnp.concatenate([theirs0, theirs1], 0).astype(jnp.bfloat16)
    pl.semaphore_wait(barrier, len(peers))
    ex = pltpu.make_async_remote_copy(src_ref=stage, dst_ref=got, send_sem=stage_sem.at[0], recv_sem=stage_sem.at[1],
                                      device_id={"tm": sib}, device_id_type=MESH)
    ex.start()

    def place(s, aa, y, bb):
        m = 2 * s + core
        blk = aa * ra + y * 4 + bb * rb
        return m, blk
    def ref_of(m, blk):
        return W.at[m, pl.ds(pl.multiple_of(blk * R, 16), R)]
    def send(s, piece, device, slot):
        m, blk = place(s, *piece)
        pltpu.make_async_remote_copy(src_ref=ref_of(m, blk), dst_ref=ref_of(m, blk), send_sem=send_sem.at[s, slot],
            recv_sem=recv_sem.at[m, blk], device_id={"tm": device}, device_id_type=MESH).start()
    def wait_blk(m, blk):
        pltpu.make_async_copy(ref_of(m, blk), ref_of(m, blk), recv_sem.at[m, blk]).wait()
    def arrive(s, piece):
        wait_blk(*place(s, *piece))
    def drain(s, slot, rows):
        pltpu.make_async_copy(W.at[0, pl.ds(0, rows)], W.at[0, pl.ds(0, rows)], send_sem.at[s, slot]).wait()

    def spread_a(s, piece):
        send(s, piece, dev_a[0], 0); send(s, piece, dev_a[1], 1)
    def spread_b(s, piece):
        send(s, piece, dev_b[0], 2); send(s, piece, dev_b[1], 3)
    def to_sib(s, piece):
        send(s, piece, sib, 4)
    ex.wait()
    g = got[...].astype(f)
    for s, mine in ((0, mine0), (1, mine1)):
        other = g[40 * s:40 * s + 40]
        both = jnp.where(flip, jnp.concatenate([mine, other], 0), jnp.concatenate([other, mine], 0))
        own[s] = both.astype(jnp.bfloat16)
    cps = []
    for s in range(2):
        m, blk = place(s, a, yh, b)
        c = pltpu.make_async_copy(own.at[s], ref_of(m, blk), local_sem.at[s]); c.start(); cps.append(c)
    for c in cps: c.wait()
    for s in range(2):
        send(s, (a, yh, b), dev_y, 5)
        spread_a(s, (a, yh, b))
    for s in range(2):
        if s == 0:
            spread_b(0, (a, yh, b))
        to_sib(s, (a, yh, b))
    def stage_a(s, with_b):
        arrive(s, (a, 1 - yh, b))
        spread_a(s, (a, 1 - yh, b))
        if with_b: spread_b(s, (a, 1 - yh, b))
        to_sib(s, (a, 1 - yh, b))
        def body(i, _):
            y = jnp.where(i == 0, yh, 1 - yh)
            d = 1 - 2 * y
            first = ring(a, -d)
            last = ring(a, d)
            arrive(s, (first, y, b))
            fwd = me + (ring(a, d) - a) * sa
            send(s, (first, y, b), fwd, y)
            if with_b: spread_b(s, (first, y, b))
            to_sib(s, (first, y, b))
            arrive(s, (last, y, b))
            if with_b: spread_b(s, (last, y, b))
            to_sib(s, (last, y, b))
            return 0
        lax.fori_loop(0, 2, body, 0)
        def body2(y, _):
            arrive(s, (ring(a, 2), y, b))
            if with_b: spread_b(s, (ring(a, 2), y, b))
            to_sib(s, (ring(a, 2), y, b))
            return 0
        lax.fori_loop(0, 2, body2, 0)
    order = lambda i: (jnp.where(i // 2 == 0, a, jnp.where(i // 2 == 1, ring(a, 1), jnp.where(i // 2 == 2, ring(a, -1), ring(a, 2)))), jnp.where(lax.rem(i, 2) == 0, yh, 1 - yh))
    def late_b(s):
        def body(i, _):
            aa, y = order(i)
            spread_b(s, (aa, y, b))
            return 0
        lax.fori_loop(0, 8, body, 0)
    def stage_b(s):
        def body(i, _):
            aa, y = order(i)
            d = 1 - 2 * y
            p1 = (aa, y, ring(b, -d)); p2 = (aa, y, ring(b, d))
            arrive(s, p1)
            send(s, p1, me + (ring(b, d) - b) * sb, 2 + y)
            to_sib(s, p1)
            arrive(s, p2)
            to_sib(s, p2)
            return 0
        lax.fori_loop(0, 8, body, 0)
    def stage_c(s):
        def body(i, _):
            aa, y = order(i)
            p = (aa, y, ring(b, 2))
            arrive(s, p); to_sib(s, p)
            return 0
        lax.fori_loop(0, 8, body, 0)
    stage_a(0, True)
    stage_a(1, False)
    stage_b(0)
    late_b(1)
    stage_c(0)
    stage_b(1)
    stage_c(1)
    def fin(i, _):
        wait_blk(2 * (i // 32) + 1 - core, lax.rem(i, 32))
        return 0
    lax.fori_loop(0, 64, fin, 0)
    for s in range(2):
        for slot, n in ((0, 3), (1, 3), (2, 12), (3, 12), (4, 32), (5, 1)):
            drain(s, slot, n * R)

def gather(wk, wv, wq, wo, vmem):
    sp = pl.BlockSpec(memory_space=pltpu.VMEM)
    return pl.pallas_call(
        gather_kernel,
        out_shape=jax.ShapeDtypeStruct((4, 2560, 1280), jnp.bfloat16),
        in_specs=[sp] * 4,
        out_specs=pl.BlockSpec(memory_space=pltpu.VMEM if vmem else pl.ANY),
        scratch_shapes=[pltpu.VMEM((2, R, 1280), jnp.bfloat16), pltpu.VMEM((R, 1280), jnp.bfloat16), pltpu.VMEM((R, 1280), jnp.bfloat16),
            pltpu.SemaphoreType.DMA((2,)), pltpu.SemaphoreType.DMA((2,)), pltpu.SemaphoreType.DMA((2, 6)), pltpu.SemaphoreType.DMA((4, 32))],
        compiler_params=pltpu.CompilerParams(collective_id=0, has_side_effects=True, vmem_limit_bytes=60 * 2**20),
    )(wk, wv, wq, wo)


def extended(block, sides, width):
    for axis, dim in sides:
        count = lax.axis_size(axis)
        forward = [(i, i + 1) for i in range(count - 1)]
        backward = [(target, source) for source, target in forward]
        low = lax.ppermute(
            lax.slice_in_dim(block, block.shape[dim] - width, None, axis=dim), axis, forward
        )
        high = lax.ppermute(lax.slice_in_dim(block, 0, width, axis=dim), axis, backward)
        block = jnp.concatenate([low, block, high], axis=dim)
    return block


def norm_pair(value, tangent, gain):
    square = jnp.mean(value * value, axis=-1, keepdims=True) + eps
    factor = lax.rsqrt(square)
    inner = jnp.mean(value * tangent, axis=-1, keepdims=True)
    return (
        value * factor * gain,
        (tangent * factor - value * (factor * factor * factor) * inner) * gain,
    )


def window_mask(query_place, key_place, total):
    offset = query_place[:, None] - key_place[None, :]
    inside = (key_place[None, :] >= 0) & (key_place[None, :] < total)
    return (offset <= WIN) & (offset >= -WIN) & inside


def attend(query, query_tan, keys, keys_tan, values, values_tan, valid):
    scale = 1.0 / math.sqrt(query.shape[-1])
    scores = jnp.einsum("qhd,khd->hqk", query, keys, preferred_element_type=jnp.float32) * scale
    weights = jnp.where(valid, jnp.exp(scores), 0.0)
    weights = weights / jnp.sum(weights, axis=-1, keepdims=True)
    scores_tan = (
        jnp.einsum("pqhd,khd->phqk", query_tan, keys, preferred_element_type=jnp.float32)
        + jnp.einsum("qhd,pkhd->phqk", query, keys_tan, preferred_element_type=jnp.float32)
    ) * scale
    scores_tan = jnp.where(valid, scores_tan, 0.0)
    weights_tan = weights * (scores_tan - jnp.sum(weights * scores_tan, axis=-1, keepdims=True))
    weights_low = weights.astype(jnp.bfloat16)
    weights_tan_low = weights_tan.astype(jnp.bfloat16)
    output = jnp.einsum("hqk,khd->qhd", weights_low, values, preferred_element_type=jnp.float32)
    output_tan = jnp.einsum(
        "phqk,khd->pqhd", weights_tan_low, values, preferred_element_type=jnp.float32
    ) + jnp.einsum("hqk,pkhd->pqhd", weights_low, values_tan, preferred_element_type=jnp.float32)
    return (output.astype(jnp.bfloat16), output_tan.astype(jnp.bfloat16))


def shards(tokens, probes, norm_gain, w_query, w_key, w_value, query_gain, key_gain, w_out):
    probe_count = probes.shape[0]
    seq_rows = tokens.shape[0]
    width = tokens.shape[1]
    section = w_query.shape[1]
    head_count = section // HEAD_DIM
    value = tokens.astype(jnp.float32)
    tangent = probes.astype(jnp.float32)
    normed, normed_tan = norm_pair(value, tangent, norm_gain)
    rows_all = (
        jnp.concatenate([normed[None], normed_tan], 0)
        .astype(jnp.bfloat16)
        .reshape((probe_count + 1) * seq_rows, width)
    )

    def add_rows(piece):
        return jnp.dot(rows_all, piece, preferred_element_type=jnp.float32)

    def norm_heads(flat, gain):
        full = flat.reshape(probe_count + 1, seq_rows, head_count, HEAD_DIM)
        normal, normal_tan = norm_pair(full[0], full[1:], gain.reshape(head_count, HEAD_DIM))
        return (normal.astype(jnp.bfloat16), normal_tan.astype(jnp.bfloat16))

    whole = gather(w_key, w_value, w_query, w_out, False)
    pieces = (whole[2], whole[0], whole[1])
    query_flat = add_rows(pieces[0])
    key_flat = add_rows(pieces[1])
    value_flat = add_rows(pieces[2])
    keys, keys_tan = norm_heads(key_flat, key_gain)
    value_low = value_flat.astype(jnp.bfloat16).reshape(probe_count + 1, seq_rows, section)
    pieces = [keys.reshape(seq_rows, section)]
    pieces = pieces + [keys_tan[index].reshape(seq_rows, section) for index in range(probe_count)]
    pieces = pieces + [value_low[index] for index in range(probe_count + 1)]
    packed = jnp.concatenate(pieces, 1)
    margin = extended(packed, (("tm", 0),), WIN)
    query, query_tan = norm_heads(query_flat, query_gain)
    span = margin.shape[0]
    stacked = margin.reshape(span, 2 * (probe_count + 1), head_count, HEAD_DIM)
    keys = stacked[:, 0]
    keys_tan = jnp.moveaxis(stacked[:, 1 : probe_count + 1], 1, 0)
    values = stacked[:, probe_count + 1]
    values_tan = jnp.moveaxis(stacked[:, probe_count + 2 :], 1, 0)
    start_row = lax.axis_index("tm") * seq_rows
    query_place = start_row + jnp.arange(seq_rows, dtype=jnp.int32)
    key_place = start_row - WIN + jnp.arange(span, dtype=jnp.int32)
    valid = window_mask(query_place, key_place, seq_rows * lax.axis_size("tm"))
    output, output_tan = attend(query, query_tan, keys, keys_tan, values, values_tan, valid)
    out_rows = jnp.concatenate(
        [output.reshape(1, seq_rows, section), output_tan.reshape(probe_count, seq_rows, section)],
        0,
    ).reshape((probe_count + 1) * seq_rows, section)
    terms = lax.dot_general(
        out_rows, whole[3], (((1,), (1,)), ((), ())), preferred_element_type=jnp.float32
    )
    part_width = width // 2
    side = lax.axis_index("segment")
    away = lax.dynamic_slice_in_dim(terms[:seq_rows], (1 - side) * part_width, part_width, 1)
    near = lax.dynamic_slice_in_dim(terms[:seq_rows], side * part_width, part_width, 1)
    share = lax.ppermute(away.astype(jnp.bfloat16), "segment", [(0, 1), (1, 0)])
    velocity = (near + share.astype(jnp.float32)).astype(jnp.bfloat16)
    total = jnp.sum(
        tangent * terms[seq_rows:].reshape(probe_count, seq_rows, width), axis=(0, 2)
    )
    total = total + lax.ppermute(total, "segment", [(0, 1), (1, 0)])
    density = total / (probe_count * math.sqrt(width))
    return (velocity, density)


def solution(mesh):
    placed = (
        P("tm", None),
        P(None, "tm", None),
        P(),
        P("tm", "segment"),
        P("tm", "segment"),
        P("tm", "segment"),
        P("segment"),
        P("segment"),
        P("tm", "segment"),
    )
    return jax.shard_map(
        shards, mesh=mesh, in_specs=placed, out_specs=(P("tm", "segment"), P("tm")), check_vma=False
    )
```

```python
import math

import jax
import jax.numpy as jnp
from jax import lax
from jax.experimental import pallas as pl
from jax.experimental.pallas import tpu as pltpu
from jax.sharding import PartitionSpec as P

MESH = pl.DeviceIdType.MESH
HEAD = 128
WIN = 128
EPS = 1e-06
BF = jnp.bfloat16
F32 = jnp.float32

ROWS = 256
WIDTH = 2560
SEC = 1280
HALF = 640
PIECE = 80
HEADS = 10
ROW_BLOCK = 16

UNITS = 3


def norm_pair(value, tangents, gain):
    factor = lax.rsqrt(jnp.mean(value * value, axis=-1, keepdims=True) + EPS)
    cube = factor * factor * factor
    outs = [value * factor * gain]
    for tangent in tangents:
        inner = jnp.mean(value * tangent, axis=-1, keepdims=True)
        outs.append((tangent * factor - value * (cube * inner)) * gain)
    return outs


def kernel(
    tokens_hbm, probes_hbm, gain_ref, wq, wk, wv, wo, qgain, kgain,
    velocity_ref, density_ref,
    W, tokens, probes, h, ext, q, o, near, away, share, dens, dens_in,
    own_kv, own_q, own_o, stage, got,
    in_sem, stage_sem, local_sem, y_sem, send_sem, pair_sem, opp_sem, sib_sem, halo_send, halo_recv, out_sem,
):
    me = lax.axis_index("tm")
    side = lax.axis_index("segment")
    core = lax.rem(me, 2)
    x = lax.rem(me // 2, 4)
    yh = lax.rem(me // 8, 2)
    z = me // 16
    flip = core == 0
    a = jnp.where(flip, x, z)
    b = jnp.where(flip, z, x)
    sa = jnp.where(flip, 2, 16)
    sb = jnp.where(flip, 16, 2)

    def ring(p, d):
        return lax.rem(p + d + 4, 4)

    dev_a = [me + (ring(a, d) - a) * sa for d in (1, -1)]
    dev_b = [me + (ring(b, d) - b) * sb for d in (1, -1)]
    sib = me + 1 - 2 * core
    far = lax.rem(me + 2 * core - 1 + 64, 64)
    dev_y = me + (1 - 2 * yh) * 8

    barrier = pltpu.get_barrier_semaphore()
    peers = [sib, dev_y, *dev_a, *dev_b, far]
    for d in peers:
        pl.semaphore_signal(barrier, inc=1, device_id={"tm": d}, device_id_type=MESH)
    pl.semaphore_signal(barrier, inc=1, device_id={"segment": 1 - side}, device_id_type=MESH)

    load_tokens = pltpu.make_async_copy(tokens_hbm, tokens, in_sem.at[0])
    load_probes = pltpu.make_async_copy(probes_hbm, probes, in_sem.at[1])
    load_tokens.start()
    load_probes.start()

    k_rows, v_rows = wk[...].astype(F32), wv[...].astype(F32)
    q_rows, o_rows = wq[...].astype(F32), wo[...].astype(F32)
    mine_kv = jnp.where(flip, k_rows, v_rows)
    theirs_kv = jnp.where(flip, v_rows, k_rows)
    mine_qo = jnp.where(
        flip,
        jnp.concatenate([q_rows[:, :HALF], o_rows[:, :HALF]], 1),
        jnp.concatenate([q_rows[:, HALF:], o_rows[:, HALF:]], 1),
    )
    theirs_qo = jnp.where(
        flip,
        jnp.concatenate([q_rows[:, HALF:], o_rows[:, HALF:]], 1),
        jnp.concatenate([q_rows[:, :HALF], o_rows[:, :HALF]], 1),
    )
    stage[...] = jnp.concatenate([theirs_kv, theirs_qo], 0).astype(BF)
    pl.semaphore_wait(barrier, len(peers) + 1)
    swap = pltpu.make_async_remote_copy(
        src_ref=stage, dst_ref=got, send_sem=stage_sem.at[0], recv_sem=stage_sem.at[1],
        device_id={"tm": sib}, device_id_type=MESH,
    )
    swap.start()
    swap.wait()
    theirs = got[...].astype(F32)

    def both(mine, other):
        return jnp.where(
            flip, jnp.concatenate([mine, other], 0), jnp.concatenate([other, mine], 0)
        ).astype(BF)

    own_kv[...] = both(mine_kv, theirs[:40])
    qo = both(mine_qo, theirs[40:])
    own_q[...] = qo[:, :HALF]
    own_o[...] = qo[:, HALF:]

    def columns(s):
        if s == 0:
            return pl.ds(0, SEC)
        return pl.ds(pl.multiple_of(core * HALF, 128), HALF)

    def matrix(s, c):
        return c if s == 0 else s + 1

    def place(aa, bb):
        return jnp.where(flip, bb, aa), jnp.where(flip, aa, bb)

    def pair(s, aa, bb):
        zz, xx = place(aa, bb)
        return W.at[matrix(s, core), zz, :, xx, :, columns(s)]

    def single(s, aa, y, bb):
        zz, xx = place(aa, bb)
        return W.at[matrix(s, core), zz, y, xx, :, columns(s)]

    def send(ref, send_to, recv, device):
        pltpu.make_async_remote_copy(
            src_ref=ref, dst_ref=ref, send_sem=send_to, recv_sem=recv,
            device_id={"tm": device}, device_id_type=MESH,
        ).start()

    def await_ref(ref, sem):
        pltpu.make_async_copy(ref, ref, sem).wait()

    def send_pair(s, which, aa, bb):
        devs = dev_a if which == 0 else dev_b
        for k in range(2):
            send(pair(s, aa, bb), send_sem.at[s, which, k], pair_sem.at[s, aa, bb], devs[k])

    def send_opp(s, which, y, aa, bb):
        devs = dev_a if which == 0 else dev_b
        send(single(s, aa, y, bb), send_sem.at[s, which, y], opp_sem.at[s, y, aa, bb], devs[y])

    def to_sib(s, aa, bb):
        zz, xx = place(aa, bb)
        send(pair(s, aa, bb), send_sem.at[s, 2, 0], sib_sem.at[s, zz, xx], sib)

    def await_pair(s, aa, bb):
        await_ref(pair(s, aa, bb), pair_sem.at[s, aa, bb])

    def await_opp(s, aa, bb):
        for y in range(2):
            await_ref(single(s, aa, y, bb), opp_sem.at[s, y, aa, bb])

    def order(i):
        return jnp.where(i == 0, a, jnp.where(i == 1, ring(a, 1), jnp.where(i == 2, ring(a, -1), ring(a, 2))))

    owns = (own_kv, own_q, own_o)
    for s in range(UNITS):
        pltpu.make_async_copy(owns[s], single(s, a, yh, b), local_sem.at[s]).start()
    for s in range(UNITS):
        pltpu.make_async_copy(owns[s], single(s, a, yh, b), local_sem.at[s]).wait()
        send(single(s, a, yh, b), y_sem.at[s, 0], y_sem.at[s, 1], dev_y)
    for s in range(UNITS):
        await_ref(single(s, a, 1 - yh, b), y_sem.at[s, 1])
        send_pair(s, 0, a, b)
        if s == 0:
            send_pair(0, 1, a, b)
        to_sib(s, a, b)
    for s in range(UNITS):
        await_pair(s, ring(a, -1), b)
        send_opp(s, 0, 0, ring(a, -1), b)
        await_pair(s, ring(a, 1), b)
        send_opp(s, 0, 1, ring(a, 1), b)
        if s == 0:
            send_pair(0, 1, ring(a, 1), b)
            send_pair(0, 1, ring(a, -1), b)
        to_sib(s, ring(a, 1), b)
        to_sib(s, ring(a, -1), b)
    for s in range(UNITS):
        await_opp(s, ring(a, 2), b)
        if s == 0:
            send_pair(0, 1, ring(a, 2), b)
        to_sib(s, ring(a, 2), b)

    def start_b(s):
        for i in range(4):
            send_pair(s, 1, order(i), b)

    def pass_b(s, i):
        aa = order(i)
        await_pair(s, aa, ring(b, -1))
        send_opp(s, 1, 0, aa, ring(b, -1))
        to_sib(s, aa, ring(b, -1))
        await_pair(s, aa, ring(b, 1))
        send_opp(s, 1, 1, aa, ring(b, 1))
        to_sib(s, aa, ring(b, 1))

    def end_b(s, i):
        aa = order(i)
        await_opp(s, aa, ring(b, 2))
        to_sib(s, aa, ring(b, 2))

    def await_sib(s):
        def body(i, _):
            zz, xx = i // 4, lax.rem(i, 4)
            if s == 0:
                ref = W.at[1 - core, zz, :, xx]
            else:
                ref = W.at[s + 1, zz, :, xx, :, pl.ds(pl.multiple_of((1 - core) * HALF, 128), HALF)]
            await_ref(ref, sib_sem.at[s, zz, xx])
            return 0

        lax.fori_loop(0, 16, body, 0)

    load_tokens.wait()
    load_probes.wait()

    def norm_block(i):
        rows = pl.ds(pl.multiple_of(i * ROW_BLOCK, ROW_BLOCK), ROW_BLOCK)
        outs = norm_pair(
            tokens[rows].astype(F32), [probes[p, rows].astype(F32) for p in range(2)], gain_ref[...]
        )
        for p in range(3):
            h[p, rows] = outs[p].astype(BF)

    def first(i, _):
        lax.fori_loop(0, 4, lambda j, c: (norm_block(i * 4 + j), c)[1], 0)
        pass_b(0, i)
        return 0

    lax.fori_loop(0, 4, first, 0)
    start_b(1)
    lax.fori_loop(0, 4, lambda i, c: (end_b(0, i), c)[1], 0)
    await_sib(0)

    def project(m, n):
        cols = pl.ds(pl.multiple_of(n * 256, 256), 256)
        weight = W[m, :, :, :, :, cols].reshape(WIDTH, 256)
        return jnp.dot(
            h[...].reshape(3 * ROWS, WIDTH), weight, preferred_element_type=F32
        ).reshape(3, ROWS, 256)

    def heads_out(res, gain_ref_, n, dst, base, offset):
        for j in range(2):
            cols = pl.ds(pl.multiple_of(n * 256 + j * 128, 128), 128)
            part = res[:, :, j * 128:(j + 1) * 128]
            outs = norm_pair(part[0], [part[1], part[2]], gain_ref_[:, cols])
            for p in range(3):
                dst[base + p, pl.ds(offset, ROWS), cols] = outs[p].astype(BF)

    def halo(base, which):
        last = (core + which) == 0
        last = jnp.logical_or(last, (core + which) == 2)
        src = jnp.where(last, 2 * WIN, WIN)
        dst = jnp.where(last, 0, 3 * WIN)
        device = sib if which == 0 else far
        return pltpu.make_async_remote_copy(
            src_ref=ext.at[pl.ds(base, 3), pl.ds(pl.multiple_of(src, WIN), WIN)],
            dst_ref=ext.at[pl.ds(base, 3), pl.ds(pl.multiple_of(dst, WIN), WIN)],
            send_sem=halo_send.at[base // 3, which], recv_sem=halo_recv.at[base // 3, which],
            device_id={"tm": device}, device_id_type=MESH,
        )

    def key_tile(n, _):
        heads_out(project(0, n), kgain, n, ext, 0, WIN)
        return 0

    lax.fori_loop(0, 5, key_tile, 0)
    for which in (1, 0):
        halo(0, which).start()

    def value_tile(n, _):
        res = project(1, n)
        cols = pl.ds(pl.multiple_of(n * 256, 256), 256)
        for p in range(3):
            ext[3 + p, pl.ds(WIN, ROWS), cols] = res[p].astype(BF)

        @pl.when(n < 4)
        def _():
            pass_b(1, n)

        return 0

    lax.fori_loop(0, 5, value_tile, 0)
    for which in (1, 0):
        halo(3, which).start()
    start_b(2)
    lax.fori_loop(0, 4, lambda i, c: (end_b(1, i), c)[1], 0)
    await_sib(1)

    def query_tile(n, _):
        heads_out(project(2, n), qgain, n, q, 0, 0)

        @pl.when(n < 4)
        def _():
            pass_b(2, n)

        return 0

    lax.fori_loop(0, 5, query_tile, 0)
    for base in (0, 3):
        for which in (1, 0):
            halo(base, which).wait()

    scale = 1.0 / math.sqrt(HEAD)
    u = lax.broadcasted_iota(jnp.int32, (WIN, 3 * WIN), 0)
    w = lax.broadcasted_iota(jnp.int32, (WIN, 3 * WIN), 1)
    band = (w - u >= 0) & (w - u <= 2 * WIN)
    NT = (((1,), (1,)), ((), ()))

    def attend(head, block):
        cols = pl.ds(pl.multiple_of(head * HEAD, HEAD), HEAD)
        rows = pl.ds(pl.multiple_of(block * WIN, WIN), WIN)
        keys = pl.ds(pl.multiple_of(block * WIN, WIN), 3 * WIN)
        place_ = me * ROWS - WIN + block * WIN + w
        valid = band & (place_ >= 0) & (place_ < 64 * ROWS)
        qn, dq0, dq1 = [q[p, rows, cols] for p in range(3)]
        k, dk0, dk1, v, dv0, dv1 = [ext[p, keys, cols] for p in range(6)]
        zero = jnp.zeros_like(qn)
        left = jnp.concatenate(
            [jnp.concatenate([qn, zero], 1), jnp.concatenate([dq0, qn], 1)], 0
        )
        first_ = lax.dot_general(left, jnp.concatenate([k, dk0], 1), NT, preferred_element_type=F32)
        second = lax.dot_general(
            jnp.concatenate([dq1, qn], 1), jnp.concatenate([k, dk1], 1), NT, preferred_element_type=F32
        )
        e = jnp.where(valid, jnp.exp(first_[:WIN] * scale), 0.0)
        weights = e * (1.0 / jnp.sum(e, axis=-1, keepdims=True))
        tans = []
        for ds in (first_[WIN:], second):
            ds = jnp.where(valid, ds * scale, 0.0)
            tans.append(weights * (ds - jnp.sum(weights * ds, axis=-1, keepdims=True)))
        low = weights.astype(BF)
        stack = jnp.concatenate([low, tans[0].astype(BF), tans[1].astype(BF)], 0)
        by_v = jnp.dot(stack, v, preferred_element_type=F32)
        by_dv = jnp.dot(low, jnp.concatenate([dv0, dv1], 1), preferred_element_type=F32)
        o[0, rows, cols] = by_v[:WIN].astype(BF)
        o[1, rows, cols] = (by_v[WIN:2 * WIN] + by_dv[:, :HEAD]).astype(BF)
        o[2, rows, cols] = (by_v[2 * WIN:] + by_dv[:, HEAD:]).astype(BF)

    def attend_step(i, _):
        attend(i // 2, lax.rem(i, 2))

        @pl.when(i < 4)
        def _():
            end_b(2, i)

        return 0

    lax.fori_loop(0, 2 * HEADS, attend_step, 0)
    await_sib(2)

    def out_rows(p, half):
        weight = W[3, pl.ds(2 * half, 2)].reshape(SEC, SEC)
        return lax.dot_general(o[p], weight, NT, preferred_element_type=F32)

    away[...] = out_rows(0, 1 - side).astype(BF)
    give = pltpu.make_async_remote_copy(
        src_ref=away, dst_ref=share, send_sem=out_sem.at[0], recv_sem=out_sem.at[1],
        device_id={"segment": 1 - side}, device_id_type=MESH,
    )
    give.start()
    near[...] = out_rows(0, side)

    dens[...] = jnp.zeros_like(dens)

    def trace_step(i, _):
        p, half = i // 2, lax.rem(i, 2)
        dy = out_rows(1 + p, half)
        prod = dy * probes[p, :, pl.ds(pl.multiple_of(half * SEC, SEC), SEC)].astype(F32)
        total = prod[:, :128]
        for j in range(1, SEC // 128):
            total = total + prod[:, j * 128:(j + 1) * 128]
        dens[...] += jnp.sum(total.T, axis=0, keepdims=True)
        return 0

    lax.fori_loop(0, 4, trace_step, 0)
    give_dens = pltpu.make_async_remote_copy(
        src_ref=dens, dst_ref=dens_in, send_sem=out_sem.at[2], recv_sem=out_sem.at[3],
        device_id={"segment": 1 - side}, device_id_type=MESH,
    )
    give_dens.start()
    give.wait()
    velocity_ref[...] = (near[...] + share[...].astype(F32)).astype(BF)
    give_dens.wait()
    density_ref[...] = (dens[...] + dens_in[...]) * (1.0 / (2 * math.sqrt(WIDTH)))

    for s in range(UNITS):
        await_ref(single(s, a, yh, b), y_sem.at[s, 0])
        for k in range(2):
            for which in range(2):
                n = 3 if which == 0 else 12
                ref = W.at[0].at[pl.ds(0, 1), 0, pl.ds(0, 3)] if n == 3 else W.at[0].at[:, 0, pl.ds(0, 3)]
                ref = ref.at[:, :, :, columns(s)]
                await_ref(ref, send_sem.at[s, which, k])
        await_ref(W.at[0].at[:, :, :, :, columns(s)], send_sem.at[s, 2, 0])


def layer(tokens, probes, norm_gain, w_query, w_key, w_value, query_gain, key_gain, w_out):
    vmem = pl.BlockSpec(memory_space=pltpu.VMEM)
    hbm = pl.BlockSpec(memory_space=pl.ANY)
    V, D, R = pltpu.VMEM, pltpu.SemaphoreType.DMA, None
    velocity, density = pl.pallas_call(
        kernel,
        out_shape=(
            jax.ShapeDtypeStruct((ROWS, SEC), BF),
            jax.ShapeDtypeStruct((8, ROWS), F32),
        ),
        in_specs=[hbm, hbm] + [vmem] * 7,
        out_specs=(vmem, vmem),
        scratch_shapes=[
            V((4, 4, 2, 4, PIECE, SEC), BF),
            V((ROWS, WIDTH), BF),
            V((2, ROWS, WIDTH), jnp.int32),
            V((3, ROWS, WIDTH), BF),
            V((6, ROWS + 2 * WIN, SEC), BF),
            V((3, ROWS, SEC), BF),
            V((3, ROWS, SEC), BF),
            V((ROWS, SEC), F32),
            V((ROWS, SEC), BF),
            V((ROWS, SEC), BF),
            V((8, ROWS), F32),
            V((8, ROWS), F32),
            V((PIECE, SEC), BF),
            V((PIECE, HALF), BF),
            V((PIECE, HALF), BF),
            V((PIECE, SEC), BF),
            V((PIECE, SEC), BF),
            D((2,)), D((2,)), D((UNITS,)), D((UNITS, 2)), D((UNITS, 3, 2)),
            D((UNITS, 4, 4)), D((UNITS, 2, 4, 4)), D((UNITS, 4, 4)),
            D((2, 2)), D((2, 2)), D((4,)),
        ],
        compiler_params=pltpu.CompilerParams(
            collective_id=0, has_side_effects=True, vmem_limit_bytes=60 * 2**20
        ),
    )(
        tokens, probes, norm_gain.reshape(1, -1), w_query, w_key, w_value, w_out,
        query_gain.reshape(1, -1), key_gain.reshape(1, -1),
    )
    return velocity, density[0]


def solution(mesh):
    placed = (
        P("tm", None),
        P(None, "tm", None),
        P(),
        P("tm", "segment"),
        P("tm", "segment"),
        P("tm", "segment"),
        P("segment"),
        P("segment"),
        P("tm", "segment"),
    )
    return jax.shard_map(
        layer, mesh=mesh, in_specs=placed, out_specs=(P("tm", "segment"), P("tm")), check_vma=False
    )
```

```python
import math

import jax
import jax.numpy as jnp
from jax import lax
from jax.experimental import pallas as pl
from jax.experimental.pallas import tpu as pltpu
from jax.sharding import PartitionSpec as P

MESH = pl.DeviceIdType.MESH
HEAD = 128
WIN = 128
EPS = 1e-06
BF = jnp.bfloat16
F32 = jnp.float32

ROWS = 256
WIDTH = 2560
SEC = 1280
HALF = 640
PIECE = 80
HEADS = 10
ROW_BLOCK = 16

UNITS = 4


def norm_pair(value, tangents, gain):
    factor = lax.rsqrt(jnp.mean(value * value, axis=-1, keepdims=True) + EPS)
    cube = factor * factor * factor
    outs = [value * factor * gain]
    for tangent in tangents:
        inner = jnp.mean(value * tangent, axis=-1, keepdims=True)
        outs.append((tangent * factor - value * (cube * inner)) * gain)
    return outs


def kernel(
    tokens_hbm, probes_hbm, gain_ref, wq, wk, wv, wo, qgain, kgain,
    velocity_ref, density_ref,
    W, tokens, probes, h, ext, q, o, near, away, share, dens, dens_in,
    own, stage, got,
    in_sem, stage_sem, local_sem, y_sem, send_sem, pair_sem, opp_sem, sib_sem, halo_send, halo_recv, out_sem,
):
    me = lax.axis_index("tm")
    side = lax.axis_index("segment")
    core = lax.rem(me, 2)
    x = lax.rem(me // 2, 4)
    yh = lax.rem(me // 8, 2)
    z = me // 16
    flip = core == 0

    def ring(p, d):
        return lax.rem(p + d + 4, 4)

    dev_x = [me + (ring(x, d) - x) * 2 for d in (1, -1)]
    dev_z = [me + (ring(z, d) - z) * 16 for d in (1, -1)]
    by_core = (
        jnp.where(flip, x, z),
        jnp.where(flip, z, x),
        [jnp.where(flip, i, j) for i, j in zip(dev_x, dev_z)],
        [jnp.where(flip, j, i) for i, j in zip(dev_x, dev_z)],
    )
    A, B, DEV_A, DEV_B = zip(*[by_core] * UNITS)
    sib = me + 1 - 2 * core
    far = lax.rem(me + 2 * core - 1 + 64, 64)
    dev_y = me + (1 - 2 * yh) * 8

    barrier = pltpu.get_barrier_semaphore()
    peers = [sib, dev_y, *dev_x, *dev_z, far]
    for d in peers:
        pl.semaphore_signal(barrier, inc=1, device_id={"tm": d}, device_id_type=MESH)
    pl.semaphore_signal(barrier, inc=1, device_id={"segment": 1 - side}, device_id_type=MESH)

    load_tokens = pltpu.make_async_copy(tokens_hbm, tokens, in_sem.at[0])
    load_probes = pltpu.make_async_copy(probes_hbm, probes, in_sem.at[1])
    load_tokens.start()
    load_probes.start()

    k_rows, v_rows = wk[...].astype(F32), wv[...].astype(F32)
    q_rows, o_rows = wq[...].astype(F32), wo[...].astype(F32)
    def halves(one, two):
        low = jnp.concatenate([one[:, :HALF], two[:, :HALF]], 1)
        high = jnp.concatenate([one[:, HALF:], two[:, HALF:]], 1)
        return jnp.where(flip, low, high), jnp.where(flip, high, low)

    mine_kv, theirs_kv = halves(k_rows, v_rows)
    mine_qo, theirs_qo = halves(q_rows, o_rows)
    stage[...] = jnp.concatenate([theirs_kv, theirs_qo], 0).astype(BF)
    pl.semaphore_wait(barrier, len(peers) + 1)
    swap = pltpu.make_async_remote_copy(
        src_ref=stage, dst_ref=got, send_sem=stage_sem.at[0], recv_sem=stage_sem.at[1],
        device_id={"tm": sib}, device_id_type=MESH,
    )
    swap.start()
    swap.wait()
    theirs = got[...].astype(F32)

    def both(mine, other):
        return jnp.where(
            flip, jnp.concatenate([mine, other], 0), jnp.concatenate([other, mine], 0)
        ).astype(BF)

    kv = both(mine_kv, theirs[:40])
    qo = both(mine_qo, theirs[40:])
    own[0] = kv[:, :HALF]
    own[1] = kv[:, HALF:]
    own[2] = qo[:, :HALF]
    own[3] = qo[:, HALF:]
    my_cols = pl.ds(pl.multiple_of(core * HALF, 128), HALF)
    sib_cols = pl.ds(pl.multiple_of((1 - core) * HALF, 128), HALF)

    def place(s, aa, bb):
        return jnp.where(flip, bb, aa), jnp.where(flip, aa, bb)

    def pair(s, aa, bb):
        zz, xx = place(s, aa, bb)
        return W.at[s, zz, :, xx, :, my_cols]

    def single(s, aa, y, bb):
        zz, xx = place(s, aa, bb)
        return W.at[s, zz, y, xx, :, my_cols]

    def send(ref, send_to, recv, device):
        pltpu.make_async_remote_copy(
            src_ref=ref, dst_ref=ref, send_sem=send_to, recv_sem=recv,
            device_id={"tm": device}, device_id_type=MESH,
        ).start()

    def await_ref(ref, sem):
        pltpu.make_async_copy(ref, ref, sem).wait()

    def send_pair(s, which, aa, bb):
        devs = DEV_A[s] if which == 0 else DEV_B[s]
        for k in range(2):
            send(pair(s, aa, bb), send_sem.at[s, which, k], pair_sem.at[s, aa, bb], devs[k])

    def send_single(s, which, y):
        devs = DEV_A[s] if which == 0 else DEV_B[s]
        for k in range(2):
            send(single(s, A[s], y, B[s]), send_sem.at[s, which, k], pair_sem.at[s, A[s], B[s]], devs[k])

    def send_opp(s, which, y, aa, bb):
        devs = DEV_A[s] if which == 0 else DEV_B[s]
        send(single(s, aa, y, bb), send_sem.at[s, which, y], opp_sem.at[s, y, aa, bb], devs[y])

    def to_sib(s, aa, bb):
        zz, xx = place(s, aa, bb)
        send(pair(s, aa, bb), send_sem.at[s, 2, 0], sib_sem.at[s, zz, xx], sib)

    def await_pair(s, aa, bb):
        await_ref(pair(s, aa, bb), pair_sem.at[s, aa, bb])

    def await_opp(s, aa, bb):
        for y in range(2):
            await_ref(single(s, aa, y, bb), opp_sem.at[s, y, aa, bb])

    def order(s, i):
        a = A[s]
        return jnp.where(i == 0, a, jnp.where(i == 1, ring(a, 1), jnp.where(i == 2, ring(a, -1), ring(a, 2))))

    for s in range(UNITS):
        pltpu.make_async_copy(own.at[s], single(s, A[s], yh, B[s]), local_sem.at[s]).start()
    for s in range(UNITS):
        pltpu.make_async_copy(own.at[s], single(s, A[s], yh, B[s]), local_sem.at[s]).wait()
        send(single(s, A[s], yh, B[s]), y_sem.at[s, 0], y_sem.at[s, 1], dev_y)
        send_single(s, 0, yh)
        if s == 0:
            send_single(0, 1, yh)
    load_tokens.wait()
    load_probes.wait()

    def norm_block(i):
        rows = pl.ds(pl.multiple_of(i * ROW_BLOCK, ROW_BLOCK), ROW_BLOCK)
        outs = norm_pair(
            tokens[rows].astype(F32), [probes[p, rows].astype(F32) for p in range(2)], gain_ref[...].reshape(1, WIDTH)
        )
        for p in range(3):
            h[p, rows] = outs[p].astype(BF)

    lax.fori_loop(0, ROWS // ROW_BLOCK, lambda i, c: (norm_block(i), c)[1], 0)
    part = pl.ds(pl.multiple_of(side * SEC, SEC), SEC)
    outer = pltpu.make_async_remote_copy(
        src_ref=h.at[:, pl.ds(pl.multiple_of(core * WIN, WIN), WIN), part],
        dst_ref=h.at[:, pl.ds(ROWS, WIN), part],
        send_sem=halo_send.at[2], recv_sem=halo_recv.at[2], device_id={"tm": far}, device_id_type=MESH,
    )
    relay = pltpu.make_async_remote_copy(
        src_ref=h.at[:, pl.ds(ROWS, WIN), part], dst_ref=h.at[:, pl.ds(ROWS, WIN), part],
        send_sem=halo_send.at[3], recv_sem=halo_recv.at[3], device_id={"segment": 1 - side}, device_id_type=MESH,
    )
    outer.start()

    for s in range(UNITS):
        await_ref(single(s, A[s], 1 - yh, B[s]), y_sem.at[s, 1])
        send_single(s, 0, 1 - yh)
        if s == 0:
            send_single(0, 1, 1 - yh)
        to_sib(s, A[s], B[s])
    for s in range(UNITS):
        a, b = A[s], B[s]
        await_pair(s, ring(a, -1), b)
        send_opp(s, 0, 0, ring(a, -1), b)
        await_pair(s, ring(a, 1), b)
        send_opp(s, 0, 1, ring(a, 1), b)
        if s == 0:
            send_pair(0, 1, ring(a, 1), b)
            send_pair(0, 1, ring(a, -1), b)
        to_sib(s, ring(a, 1), b)
        to_sib(s, ring(a, -1), b)
    for s in range(UNITS):
        a, b = A[s], B[s]
        await_opp(s, ring(a, 2), b)
        if s == 0:
            send_pair(0, 1, ring(a, 2), b)
        to_sib(s, ring(a, 2), b)

    def start_b(s):
        for i in range(4):
            send_pair(s, 1, order(s, i), B[s])

    def pass_b(s, i):
        aa, b = order(s, i), B[s]
        await_pair(s, aa, ring(b, -1))
        send_opp(s, 1, 0, aa, ring(b, -1))
        to_sib(s, aa, ring(b, -1))
        await_pair(s, aa, ring(b, 1))
        send_opp(s, 1, 1, aa, ring(b, 1))
        to_sib(s, aa, ring(b, 1))

    def end_b(s, i):
        aa, b = order(s, i), B[s]
        await_opp(s, aa, ring(b, 2))
        to_sib(s, aa, ring(b, 2))

    def await_sib(s):
        def body(i, _):
            zz, xx = i // 4, lax.rem(i, 4)
            await_ref(W.at[s, zz, :, xx, :, sib_cols], sib_sem.at[s, zz, xx])
            return 0

        lax.fori_loop(0, 16, body, 0)

    def first(i, _):
        pass_b(0, i)
        return 0

    lax.fori_loop(0, 4, first, 0)
    start_b(1)
    outer.wait()
    relay.start()
    lax.fori_loop(0, 4, lambda i, c: (end_b(0, i), c)[1], 0)
    await_sib(0)

    def project(m, n, rows):
        cols = pl.ds(pl.multiple_of(n * 256, 256), 256)
        weight = W[m, :, :, :, :, cols].reshape(WIDTH, 256)
        left = h[:, :rows].reshape(3 * rows, WIDTH)
        return jnp.dot(left, weight, preferred_element_type=F32).reshape(3, rows, 256)

    edge = pl.ds(pl.multiple_of(core * (ROWS + WIN), WIN), WIN)

    def to_ext(p, cols, rows):
        ext[p, pl.ds(WIN, ROWS), cols] = rows[:ROWS].astype(BF)
        ext[p, edge, cols] = rows[ROWS:].astype(BF)

    def to_q(p, cols, rows):
        q[p, :, cols] = rows.astype(BF)

    def heads_out(res, gain_ref_, n, write):
        for j in range(2):
            cols = pl.ds(pl.multiple_of(n * 256 + j * 128, 128), 128)
            part = res[:, :, j * 128:(j + 1) * 128]
            outs = norm_pair(part[0], [part[1], part[2]], gain_ref_[cols].reshape(1, 128))
            for p in range(3):
                write(p, cols, outs[p])

    def halo(base):
        return pltpu.make_async_remote_copy(
            src_ref=ext.at[pl.ds(base, 3), pl.ds(pl.multiple_of((2 - core) * WIN, WIN), WIN)],
            dst_ref=ext.at[pl.ds(base, 3), pl.ds(pl.multiple_of(core * (ROWS + WIN), WIN), WIN)],
            send_sem=halo_send.at[base // 3], recv_sem=halo_recv.at[base // 3],
            device_id={"tm": sib}, device_id_type=MESH,
        )

    def key_tile(n, _):
        heads_out(project(0, n, ROWS + WIN), kgain, n, to_ext)

        @pl.when(n > 0)
        def _():
            pass_b(1, n - 1)

        return 0

    relay.wait()
    lax.fori_loop(0, 5, key_tile, 0)
    halo(0).start()
    start_b(2)
    lax.fori_loop(0, 4, lambda i, c: (end_b(1, i), c)[1], 0)
    await_sib(1)

    def value_tile(n, _):
        @pl.when(n > 0)
        def _():
            pass_b(2, n - 1)

        res = project(1, n, ROWS + WIN)
        cols = pl.ds(pl.multiple_of(n * 256, 256), 256)
        for p in range(3):
            to_ext(3 + p, cols, res[p])
        return 0

    lax.fori_loop(0, 5, value_tile, 0)
    start_b(3)
    halo(3).start()
    lax.fori_loop(0, 4, lambda i, c: (end_b(2, i), c)[1], 0)
    await_sib(2)

    def query_tile(n, _):
        @pl.when(n < 4)
        def _():
            pass_b(3, n)

        heads_out(project(2, n, ROWS), qgain, n, to_q)
        return 0

    lax.fori_loop(0, 5, query_tile, 0)
    halo(0).wait()
    halo(3).wait()

    scale = 1.0 / math.sqrt(HEAD)
    u = lax.broadcasted_iota(jnp.int32, (WIN, 3 * WIN), 0)
    w = lax.broadcasted_iota(jnp.int32, (WIN, 3 * WIN), 1)
    band = (w - u >= 0) & (w - u <= 2 * WIN)
    NT = (((1,), (1,)), ((), ()))

    def attend(head, block):
        cols = pl.ds(pl.multiple_of(head * HEAD, HEAD), HEAD)
        rows = pl.ds(pl.multiple_of(block * WIN, WIN), WIN)
        keys = pl.ds(pl.multiple_of(block * WIN, WIN), 3 * WIN)
        place_ = me * ROWS - WIN + block * WIN + w
        valid = band & (place_ >= 0) & (place_ < 64 * ROWS)
        qn, dq0, dq1 = [q[p, rows, cols] for p in range(3)]
        k, dk0, dk1, v, dv0, dv1 = [ext[p, keys, cols] for p in range(6)]
        zero = jnp.zeros_like(qn)
        left = jnp.concatenate(
            [jnp.concatenate([qn, zero], 1), jnp.concatenate([dq0, qn], 1)], 0
        )
        first_ = lax.dot_general(left, jnp.concatenate([k, dk0], 1), NT, preferred_element_type=F32)
        second = lax.dot_general(
            jnp.concatenate([dq1, qn], 1), jnp.concatenate([k, dk1], 1), NT, preferred_element_type=F32
        )
        e = jnp.where(valid, jnp.exp(first_[:WIN] * scale), 0.0)
        weights = e * (1.0 / jnp.sum(e, axis=-1, keepdims=True))
        tans = []
        for ds in (first_[WIN:], second):
            ds = jnp.where(valid, ds * scale, 0.0)
            tans.append(weights * (ds - jnp.sum(weights * ds, axis=-1, keepdims=True)))
        low = weights.astype(BF)
        stack = jnp.concatenate([low, tans[0].astype(BF), tans[1].astype(BF)], 0)
        by_v = jnp.dot(stack, v, preferred_element_type=F32)
        by_dv = jnp.dot(low, jnp.concatenate([dv0, dv1], 1), preferred_element_type=F32)
        o[0, rows, cols] = by_v[:WIN].astype(BF)
        o[1, rows, cols] = (by_v[WIN:2 * WIN] + by_dv[:, :HEAD]).astype(BF)
        o[2, rows, cols] = (by_v[2 * WIN:] + by_dv[:, HEAD:]).astype(BF)

    def give(block):
        return pltpu.make_async_remote_copy(
            src_ref=away.at[block], dst_ref=share.at[block],
            send_sem=out_sem.at[block, 0], recv_sem=out_sem.at[block, 1],
            device_id={"segment": 1 - side}, device_id_type=MESH,
        )

    def out_half(left, half):
        weight = W[3, pl.ds(2 * half, 2)].reshape(SEC, SEC)
        return lax.dot_general(left, weight, NT, preferred_element_type=F32)

    def block_step(block, _):
        lax.fori_loop(0, HEADS, lambda i, c: (attend(i, block), c)[1], 0)

        @pl.when(block == 0)
        def _():
            lax.fori_loop(0, 4, lambda i, c: (end_b(3, i), c)[1], 0)
            await_sib(3)

        rows = pl.ds(pl.multiple_of(block * WIN, WIN), WIN)
        away[block] = out_half(o[0, rows], 1 - side).astype(BF)
        give(block).start()
        return 0

    lax.fori_loop(0, 2, block_step, 0)
    near[...] = out_half(o[0], side)
    dens[...] = jnp.zeros_like(dens)

    def trace_step(i, _):
        p, half = i // 2, lax.rem(i, 2)
        dy = out_half(o[1 + p], half)
        prod = dy * probes[p, :, pl.ds(pl.multiple_of(half * SEC, SEC), SEC)].astype(F32)
        total = prod[:, :128]
        for j in range(1, SEC // 128):
            total = total + prod[:, j * 128:(j + 1) * 128]
        dens[...] += jnp.sum(total.T, axis=0, keepdims=True)
        return 0

    lax.fori_loop(0, 4, trace_step, 0)
    give_dens = pltpu.make_async_remote_copy(
        src_ref=dens, dst_ref=dens_in, send_sem=out_sem.at[2, 0], recv_sem=out_sem.at[2, 1],
        device_id={"segment": 1 - side}, device_id_type=MESH,
    )
    give_dens.start()
    for block in range(2):
        give(block).wait()
        rows = pl.ds(block * WIN, WIN)
        velocity_ref[rows] = (near[rows] + share[block].astype(F32)).astype(BF)
    give_dens.wait()
    density_ref[...] = (dens[0] + dens_in[0]) * (1.0 / (2 * math.sqrt(WIDTH)))

    for s in range(UNITS):
        await_ref(single(s, A[s], yh, B[s]), y_sem.at[s, 0])
        for k in range(2):
            for which in range(2):
                n = 3 if which == 0 else 12
                ref = W.at[0].at[pl.ds(0, 1), 0, pl.ds(0, 3)] if n == 3 else W.at[0].at[:, 0, pl.ds(0, 3)]
                ref = ref.at[:, :, :, my_cols]
                await_ref(ref, send_sem.at[s, which, k])
        await_ref(W.at[0].at[:, :, :, :, my_cols], send_sem.at[s, 2, 0])


def layer(tokens, probes, norm_gain, w_query, w_key, w_value, query_gain, key_gain, w_out):
    vmem = pl.BlockSpec(memory_space=pltpu.VMEM)
    hbm = pl.BlockSpec(memory_space=pl.ANY)
    V, D, R = pltpu.VMEM, pltpu.SemaphoreType.DMA, None
    velocity, density = pl.pallas_call(
        kernel,
        out_shape=(
            jax.ShapeDtypeStruct((ROWS, SEC), BF),
            jax.ShapeDtypeStruct((ROWS,), F32),
        ),
        in_specs=[hbm, hbm] + [vmem] * 7,
        out_specs=(vmem, vmem),
        scratch_shapes=[
            V((4, 4, 2, 4, PIECE, SEC), BF),
            V((ROWS, WIDTH), BF),
            V((2, ROWS, WIDTH), jnp.int32),
            V((3, ROWS + WIN, WIDTH), BF),
            V((6, ROWS + 2 * WIN, SEC), BF),
            V((3, ROWS, SEC), BF),
            V((3, ROWS, SEC), BF),
            V((ROWS, SEC), F32),
            V((2, WIN, SEC), BF),
            V((2, WIN, SEC), BF),
            V((8, ROWS), F32),
            V((8, ROWS), F32),
            V((UNITS, PIECE, HALF), BF),
            V((PIECE, SEC), BF),
            V((PIECE, SEC), BF),
            D((2,)), D((2,)), D((UNITS,)), D((UNITS, 2)), D((UNITS, 3, 2)),
            D((UNITS, 4, 4)), D((UNITS, 2, 4, 4)), D((UNITS, 4, 4)),
            D((4,)), D((4,)), D((3, 2)),
        ],
        compiler_params=pltpu.CompilerParams(
            collective_id=0, has_side_effects=True, vmem_limit_bytes=60 * 2**20
        ),
    )(
        tokens, probes, norm_gain, w_query, w_key, w_value, w_out,
        query_gain, key_gain,
    )
    return velocity, density


def solution(mesh):
    placed = (
        P("tm", None),
        P(None, "tm", None),
        P(),
        P("tm", "segment"),
        P("tm", "segment"),
        P("tm", "segment"),
        P("segment"),
        P("segment"),
        P("tm", "segment"),
    )
    return jax.shard_map(
        layer, mesh=mesh, in_specs=placed, out_specs=(P("tm", "segment"), P("tm")), check_vma=False
    )
```

```python
import math

import jax
import jax.numpy as jnp
from jax import lax
from jax.experimental import pallas as pl
from jax.experimental.pallas import tpu as pltpu
from jax.sharding import PartitionSpec as P

MESH = pl.DeviceIdType.MESH
HEAD = 128
WIN = 128
EPS = 1e-06
BF = jnp.bfloat16
F32 = jnp.float32

ROWS = 256
WIDTH = 2560
SEC = 1280
HALF = 640
PIECE = 80
HEADS = 10
ROW_BLOCK = 16

UNITS = 4


def norm_pair(value, tangents, gain):
    factor = lax.rsqrt(jnp.mean(value * value, axis=-1, keepdims=True) + EPS)
    cube = factor * factor * factor
    outs = [value * factor * gain]
    for tangent in tangents:
        inner = jnp.mean(value * tangent, axis=-1, keepdims=True)
        outs.append((tangent * factor - value * (cube * inner)) * gain)
    return outs


def kernel(
    tokens_hbm, probes_hbm, gain_ref, wq, wk, wv, wo, qgain, kgain,
    velocity_ref, density_ref,
    W, tokens, probes, h, ext, q, o, near, away, share, dens, dens_in,
    own, stage, got,
    in_sem, stage_sem, local_sem, y_sem, send_sem, pair_sem, opp_sem, sib_sem, halo_send, halo_recv, out_sem,
):
    me = lax.axis_index("tm")
    side = lax.axis_index("segment")
    core = lax.rem(me, 2)
    x = lax.rem(me // 2, 4)
    yh = lax.rem(me // 8, 2)
    z = me // 16
    flip = core == 0

    def ring(p, d):
        return lax.rem(p + d + 4, 4)

    dev_x = [me + (ring(x, d) - x) * 2 for d in (1, -1)]
    dev_z = [me + (ring(z, d) - z) * 16 for d in (1, -1)]
    by_core = (
        jnp.where(flip, x, z),
        jnp.where(flip, z, x),
        [jnp.where(flip, i, j) for i, j in zip(dev_x, dev_z)],
        [jnp.where(flip, j, i) for i, j in zip(dev_x, dev_z)],
    )
    A, B, DEV_A, DEV_B = zip(*[by_core] * UNITS)
    sib = me + 1 - 2 * core
    far = lax.rem(me + 2 * core - 1 + 64, 64)
    dev_y = me + (1 - 2 * yh) * 8

    barrier = pltpu.get_barrier_semaphore()
    peers = [sib, dev_y, *dev_x, *dev_z, far]
    for d in peers:
        pl.semaphore_signal(barrier, inc=1, device_id={"tm": d}, device_id_type=MESH)
    pl.semaphore_signal(barrier, inc=1, device_id={"segment": 1 - side}, device_id_type=MESH)

    load_tokens = pltpu.make_async_copy(tokens_hbm, tokens, in_sem.at[0])
    load_probes = pltpu.make_async_copy(probes_hbm, probes, in_sem.at[1])
    load_tokens.start()
    load_probes.start()

    k_rows, v_rows = wk[...].astype(F32), wv[...].astype(F32)
    q_rows, o_rows = wq[...].astype(F32), wo[...].astype(F32)
    def halves(one, two):
        low = jnp.concatenate([one[:, :HALF], two[:, :HALF]], 1)
        high = jnp.concatenate([one[:, HALF:], two[:, HALF:]], 1)
        return jnp.where(flip, low, high), jnp.where(flip, high, low)

    mine_kv, theirs_kv = halves(k_rows, v_rows)
    mine_qo, theirs_qo = halves(q_rows, o_rows)
    stage[...] = jnp.concatenate([theirs_kv, theirs_qo], 0).astype(BF)
    pl.semaphore_wait(barrier, len(peers) + 1)
    swap = pltpu.make_async_remote_copy(
        src_ref=stage, dst_ref=got, send_sem=stage_sem.at[0], recv_sem=stage_sem.at[1],
        device_id={"tm": sib}, device_id_type=MESH,
    )
    swap.start()
    swap.wait()
    theirs = got[...].astype(F32)

    def both(mine, other):
        return jnp.where(
            flip, jnp.concatenate([mine, other], 0), jnp.concatenate([other, mine], 0)
        ).astype(BF)

    kv = both(mine_kv, theirs[:40])
    qo = both(mine_qo, theirs[40:])
    own[0] = kv[:, :HALF]
    own[1] = kv[:, HALF:]
    own[2] = qo[:, :HALF]
    own[3] = qo[:, HALF:]
    my_cols = pl.ds(pl.multiple_of(core * HALF, 128), HALF)
    sib_cols = pl.ds(pl.multiple_of((1 - core) * HALF, 128), HALF)

    def place(s, aa, bb):
        return jnp.where(flip, bb, aa), jnp.where(flip, aa, bb)

    def pair(s, aa, bb):
        zz, xx = place(s, aa, bb)
        return W.at[s, zz, :, xx, :, my_cols]

    def single(s, aa, y, bb):
        zz, xx = place(s, aa, bb)
        return W.at[s, zz, y, xx, :, my_cols]

    def send(ref, send_to, recv, device):
        pltpu.make_async_remote_copy(
            src_ref=ref, dst_ref=ref, send_sem=send_to, recv_sem=recv,
            device_id={"tm": device}, device_id_type=MESH,
        ).start()

    def await_ref(ref, sem):
        pltpu.make_async_copy(ref, ref, sem).wait()

    def send_pair(s, which, aa, bb):
        devs = DEV_A[s] if which == 0 else DEV_B[s]
        for k in range(2):
            send(pair(s, aa, bb), send_sem.at[s, which, k], pair_sem.at[s, aa, bb], devs[k])

    def send_single(s, which, y):
        devs = DEV_A[s] if which == 0 else DEV_B[s]
        for k in range(2):
            send(single(s, A[s], y, B[s]), send_sem.at[s, which, k], pair_sem.at[s, A[s], B[s]], devs[k])

    def send_opp(s, which, y, aa, bb):
        devs = DEV_A[s] if which == 0 else DEV_B[s]
        send(single(s, aa, y, bb), send_sem.at[s, which, y], opp_sem.at[s, y, aa, bb], devs[y])

    def to_sib(s, aa, bb):
        zz, xx = place(s, aa, bb)
        send(pair(s, aa, bb), send_sem.at[s, 2, 0], sib_sem.at[s, zz, xx], sib)

    def await_pair(s, aa, bb):
        await_ref(pair(s, aa, bb), pair_sem.at[s, aa, bb])

    def await_opp(s, aa, bb):
        for y in range(2):
            await_ref(single(s, aa, y, bb), opp_sem.at[s, y, aa, bb])

    def order(s, i):
        a = A[s]
        return jnp.where(i == 0, a, jnp.where(i == 1, ring(a, 1), jnp.where(i == 2, ring(a, -1), ring(a, 2))))

    for s in range(UNITS):
        pltpu.make_async_copy(own.at[s], single(s, A[s], yh, B[s]), local_sem.at[s]).start()
    for s in range(UNITS):
        pltpu.make_async_copy(own.at[s], single(s, A[s], yh, B[s]), local_sem.at[s]).wait()
        send(single(s, A[s], yh, B[s]), y_sem.at[s, 0], y_sem.at[s, 1], dev_y)
        send_single(s, 0, yh)
        if s == 0:
            send_single(0, 1, yh)
    load_tokens.wait()
    load_probes.wait()

    def norm_block(i):
        rows = pl.ds(pl.multiple_of(i * ROW_BLOCK, ROW_BLOCK), ROW_BLOCK)
        outs = norm_pair(
            tokens[rows].astype(F32), [probes[p, rows].astype(F32) for p in range(2)], gain_ref[...].reshape(1, WIDTH)
        )
        for p in range(3):
            h[p, rows] = outs[p].astype(BF)

    lax.fori_loop(0, ROWS // ROW_BLOCK, lambda i, c: (norm_block(i), c)[1], 0)
    part = pl.ds(pl.multiple_of(side * SEC, SEC), SEC)
    outer = pltpu.make_async_remote_copy(
        src_ref=h.at[:, pl.ds(pl.multiple_of(core * WIN, WIN), WIN), part],
        dst_ref=h.at[:, pl.ds(ROWS, WIN), part],
        send_sem=halo_send.at[2], recv_sem=halo_recv.at[2], device_id={"tm": far}, device_id_type=MESH,
    )
    relay = pltpu.make_async_remote_copy(
        src_ref=h.at[:, pl.ds(ROWS, WIN), part], dst_ref=h.at[:, pl.ds(ROWS, WIN), part],
        send_sem=halo_send.at[3], recv_sem=halo_recv.at[3], device_id={"segment": 1 - side}, device_id_type=MESH,
    )
    outer.start()

    for s in range(UNITS):
        await_ref(single(s, A[s], 1 - yh, B[s]), y_sem.at[s, 1])
        send_single(s, 0, 1 - yh)
        if s == 0:
            send_single(0, 1, 1 - yh)
        to_sib(s, A[s], B[s])
    for s in range(UNITS):
        a, b = A[s], B[s]
        await_pair(s, ring(a, -1), b)
        send_opp(s, 0, 0, ring(a, -1), b)
        await_pair(s, ring(a, 1), b)
        send_opp(s, 0, 1, ring(a, 1), b)
        if s == 0:
            send_pair(0, 1, ring(a, 1), b)
            send_pair(0, 1, ring(a, -1), b)
        to_sib(s, ring(a, 1), b)
        to_sib(s, ring(a, -1), b)
    for s in range(UNITS):
        a, b = A[s], B[s]
        await_opp(s, ring(a, 2), b)
        if s == 0:
            send_pair(0, 1, ring(a, 2), b)
        to_sib(s, ring(a, 2), b)

    def start_b(s):
        for i in range(4):
            send_pair(s, 1, order(s, i), B[s])

    def pass_b(s, i):
        aa, b = order(s, i), B[s]
        await_pair(s, aa, ring(b, -1))
        send_opp(s, 1, 0, aa, ring(b, -1))
        to_sib(s, aa, ring(b, -1))
        await_pair(s, aa, ring(b, 1))
        send_opp(s, 1, 1, aa, ring(b, 1))
        to_sib(s, aa, ring(b, 1))

    def end_b(s, i):
        aa, b = order(s, i), B[s]
        await_opp(s, aa, ring(b, 2))
        to_sib(s, aa, ring(b, 2))

    def await_sib(s):
        def body(i, _):
            zz, xx = i // 4, lax.rem(i, 4)
            await_ref(W.at[s, zz, :, xx, :, sib_cols], sib_sem.at[s, zz, xx])
            return 0

        lax.fori_loop(0, 16, body, 0)

    def first(i, _):
        pass_b(0, i)
        return 0

    lax.fori_loop(0, 4, first, 0)
    start_b(1)
    lax.fori_loop(0, 4, lambda i, c: (end_b(0, i), c)[1], 0)
    await_sib(0)

    def project(m, n, first_row, rows):
        cols = pl.ds(pl.multiple_of(n * 256, 256), 256)
        weight = W[m, :, :, :, :, cols].reshape(WIDTH, 256)
        left = h[:, first_row:first_row + rows].reshape(3 * rows, WIDTH)
        return jnp.dot(left, weight, preferred_element_type=F32).reshape(3, rows, 256)

    edge = pl.ds(pl.multiple_of(core * (ROWS + WIN), WIN), WIN)

    def to_ext(p, cols, rows):
        ext[p, pl.ds(WIN, ROWS), cols] = rows.astype(BF)

    def to_edge(p, cols, rows):
        ext[p, edge, cols] = rows.astype(BF)

    def to_q(p, cols, rows):
        q[p, :, cols] = rows.astype(BF)

    def heads_out(res, gain_ref_, n, write):
        for j in range(2):
            cols = pl.ds(pl.multiple_of(n * 256 + j * 128, 128), 128)
            part = res[:, :, j * 128:(j + 1) * 128]
            outs = norm_pair(part[0], [part[1], part[2]], gain_ref_[cols].reshape(1, 128))
            for p in range(3):
                write(p, cols, outs[p])

    def halo(base):
        return pltpu.make_async_remote_copy(
            src_ref=ext.at[pl.ds(base, 3), pl.ds(pl.multiple_of((2 - core) * WIN, WIN), WIN)],
            dst_ref=ext.at[pl.ds(base, 3), pl.ds(pl.multiple_of(core * (ROWS + WIN), WIN), WIN)],
            send_sem=halo_send.at[base // 3], recv_sem=halo_recv.at[base // 3],
            device_id={"tm": sib}, device_id_type=MESH,
        )

    def key_tile(n, _):
        heads_out(project(0, n, 0, ROWS), kgain, n, to_ext)

        @pl.when(n > 0)
        def _():
            pass_b(1, n - 1)

        return 0

    outer.wait()
    relay.start()
    lax.fori_loop(0, 5, key_tile, 0)
    halo(0).start()
    start_b(2)
    lax.fori_loop(0, 4, lambda i, c: (end_b(1, i), c)[1], 0)
    await_sib(1)

    def value_tile(n, _):
        @pl.when(n > 0)
        def _():
            pass_b(2, n - 1)

        res = project(1, n, 0, ROWS)
        cols = pl.ds(pl.multiple_of(n * 256, 256), 256)
        for p in range(3):
            to_ext(3 + p, cols, res[p])
        return 0

    lax.fori_loop(0, 5, value_tile, 0)
    start_b(3)
    halo(3).start()

    def edge_tile(n, _):
        heads_out(project(0, n, ROWS, WIN), kgain, n, to_edge)
        res = project(1, n, ROWS, WIN)
        cols = pl.ds(pl.multiple_of(n * 256, 256), 256)
        for p in range(3):
            to_edge(3 + p, cols, res[p])
        return 0

    relay.wait()
    lax.fori_loop(0, 5, edge_tile, 0)
    lax.fori_loop(0, 4, lambda i, c: (end_b(2, i), c)[1], 0)
    await_sib(2)

    def query_tile(n, _):
        @pl.when(n < 4)
        def _():
            pass_b(3, n)

        heads_out(project(2, n, 0, ROWS), qgain, n, to_q)
        return 0

    lax.fori_loop(0, 5, query_tile, 0)
    halo(0).wait()
    halo(3).wait()

    scale = 1.0 / math.sqrt(HEAD)
    u = lax.broadcasted_iota(jnp.int32, (WIN, 3 * WIN), 0)
    w = lax.broadcasted_iota(jnp.int32, (WIN, 3 * WIN), 1)
    band = (w - u >= 0) & (w - u <= 2 * WIN)
    NT = (((1,), (1,)), ((), ()))

    def attend(head, block):
        cols = pl.ds(pl.multiple_of(head * HEAD, HEAD), HEAD)
        rows = pl.ds(pl.multiple_of(block * WIN, WIN), WIN)
        keys = pl.ds(pl.multiple_of(block * WIN, WIN), 3 * WIN)
        place_ = me * ROWS - WIN + block * WIN + w
        valid = band & (place_ >= 0) & (place_ < 64 * ROWS)
        qn, dq0, dq1 = [q[p, rows, cols] for p in range(3)]
        k, dk0, dk1, v, dv0, dv1 = [ext[p, keys, cols] for p in range(6)]
        zero = jnp.zeros_like(qn)
        left = jnp.concatenate(
            [jnp.concatenate([qn, zero], 1), jnp.concatenate([dq0, qn], 1)], 0
        )
        first_ = lax.dot_general(left, jnp.concatenate([k, dk0], 1), NT, preferred_element_type=F32)
        second = lax.dot_general(
            jnp.concatenate([dq1, qn], 1), jnp.concatenate([k, dk1], 1), NT, preferred_element_type=F32
        )
        e = jnp.where(valid, jnp.exp(first_[:WIN] * scale), 0.0)
        weights = e * (1.0 / jnp.sum(e, axis=-1, keepdims=True))
        tans = []
        for ds in (first_[WIN:], second):
            ds = jnp.where(valid, ds * scale, 0.0)
            tans.append(weights * (ds - jnp.sum(weights * ds, axis=-1, keepdims=True)))
        low = weights.astype(BF)
        stack = jnp.concatenate([low, tans[0].astype(BF), tans[1].astype(BF)], 0)
        by_v = jnp.dot(stack, v, preferred_element_type=F32)
        by_dv = jnp.dot(low, jnp.concatenate([dv0, dv1], 1), preferred_element_type=F32)
        o[0, rows, cols] = by_v[:WIN].astype(BF)
        o[1, rows, cols] = (by_v[WIN:2 * WIN] + by_dv[:, :HEAD]).astype(BF)
        o[2, rows, cols] = (by_v[2 * WIN:] + by_dv[:, HEAD:]).astype(BF)

    def give(block):
        return pltpu.make_async_remote_copy(
            src_ref=away.at[block], dst_ref=share.at[block],
            send_sem=out_sem.at[block, 0], recv_sem=out_sem.at[block, 1],
            device_id={"segment": 1 - side}, device_id_type=MESH,
        )

    def out_half(left, half):
        weight = W[3, pl.ds(2 * half, 2)].reshape(SEC, SEC)
        return lax.dot_general(left, weight, NT, preferred_element_type=F32)

    def block_step(block, _):
        lax.fori_loop(0, HEADS, lambda i, c: (attend(i, block), c)[1], 0)

        @pl.when(block == 0)
        def _():
            lax.fori_loop(0, 4, lambda i, c: (end_b(3, i), c)[1], 0)
            await_sib(3)

        rows = pl.ds(pl.multiple_of(block * WIN, WIN), WIN)
        away[block] = out_half(o[0, rows], 1 - side).astype(BF)
        give(block).start()
        return 0

    lax.fori_loop(0, 2, block_step, 0)
    near[...] = out_half(o[0], side)
    dens[...] = jnp.zeros_like(dens)

    def trace_step(i, _):
        p, half = i // 2, lax.rem(i, 2)
        dy = out_half(o[1 + p], half)
        prod = dy * probes[p, :, pl.ds(pl.multiple_of(half * SEC, SEC), SEC)].astype(F32)
        total = prod[:, :128]
        for j in range(1, SEC // 128):
            total = total + prod[:, j * 128:(j + 1) * 128]
        dens[...] += jnp.sum(total.T, axis=0, keepdims=True)
        return 0

    lax.fori_loop(0, 4, trace_step, 0)
    give_dens = pltpu.make_async_remote_copy(
        src_ref=dens, dst_ref=dens_in, send_sem=out_sem.at[2, 0], recv_sem=out_sem.at[2, 1],
        device_id={"segment": 1 - side}, device_id_type=MESH,
    )
    give_dens.start()
    for block in range(2):
        give(block).wait()
        rows = pl.ds(block * WIN, WIN)
        velocity_ref[rows] = (near[rows] + share[block].astype(F32)).astype(BF)
    give_dens.wait()
    density_ref[...] = (dens[0] + dens_in[0]) * (1.0 / (2 * math.sqrt(WIDTH)))

    for s in range(UNITS):
        await_ref(single(s, A[s], yh, B[s]), y_sem.at[s, 0])
        for k in range(2):
            for which in range(2):
                n = 3 if which == 0 else 12
                ref = W.at[0].at[pl.ds(0, 1), 0, pl.ds(0, 3)] if n == 3 else W.at[0].at[:, 0, pl.ds(0, 3)]
                ref = ref.at[:, :, :, my_cols]
                await_ref(ref, send_sem.at[s, which, k])
        await_ref(W.at[0].at[:, :, :, :, my_cols], send_sem.at[s, 2, 0])


def layer(tokens, probes, norm_gain, w_query, w_key, w_value, query_gain, key_gain, w_out):
    vmem = pl.BlockSpec(memory_space=pltpu.VMEM)
    hbm = pl.BlockSpec(memory_space=pl.ANY)
    V, D, R = pltpu.VMEM, pltpu.SemaphoreType.DMA, None
    velocity, density = pl.pallas_call(
        kernel,
        out_shape=(
            jax.ShapeDtypeStruct((ROWS, SEC), BF),
            jax.ShapeDtypeStruct((ROWS,), F32),
        ),
        in_specs=[hbm, hbm] + [vmem] * 7,
        out_specs=(vmem, vmem),
        scratch_shapes=[
            V((4, 4, 2, 4, PIECE, SEC), BF),
            V((ROWS, WIDTH), BF),
            V((2, ROWS, WIDTH), jnp.int32),
            V((3, ROWS + WIN, WIDTH), BF),
            V((6, ROWS + 2 * WIN, SEC), BF),
            V((3, ROWS, SEC), BF),
            V((3, ROWS, SEC), BF),
            V((ROWS, SEC), F32),
            V((2, WIN, SEC), BF),
            V((2, WIN, SEC), BF),
            V((8, ROWS), F32),
            V((8, ROWS), F32),
            V((UNITS, PIECE, HALF), BF),
            V((PIECE, SEC), BF),
            V((PIECE, SEC), BF),
            D((2,)), D((2,)), D((UNITS,)), D((UNITS, 2)), D((UNITS, 3, 2)),
            D((UNITS, 4, 4)), D((UNITS, 2, 4, 4)), D((UNITS, 4, 4)),
            D((4,)), D((4,)), D((3, 2)),
        ],
        compiler_params=pltpu.CompilerParams(
            collective_id=0, has_side_effects=True, vmem_limit_bytes=60 * 2**20
        ),
    )(
        tokens, probes, norm_gain, w_query, w_key, w_value, w_out,
        query_gain, key_gain,
    )
    return velocity, density


def solution(mesh):
    placed = (
        P("tm", None),
        P(None, "tm", None),
        P(),
        P("tm", "segment"),
        P("tm", "segment"),
        P("tm", "segment"),
        P("segment"),
        P("segment"),
        P("tm", "segment"),
    )
    return jax.shard_map(
        layer, mesh=mesh, in_specs=placed, out_specs=(P("tm", "segment"), P("tm")), check_vma=False
    )
```

```python
import math

import jax
import jax.numpy as jnp
from jax import lax
from jax.experimental import pallas as pl
from jax.experimental.pallas import tpu as pltpu
from jax.sharding import PartitionSpec as P

MESH = pl.DeviceIdType.MESH
HEAD = 128
WIN = 128
EPS = 1e-06
BF = jnp.bfloat16
F32 = jnp.float32

ROWS = 256
WIDTH = 2560
SEC = 1280
HALF = 640
PIECE = 80
HEADS = 10
ROW_BLOCK = 16

UNITS = 4


def norm_pair(value, tangents, gain):
    factor = lax.rsqrt(jnp.mean(value * value, axis=-1, keepdims=True) + EPS)
    cube = factor * factor * factor
    outs = [value * factor * gain]
    for tangent in tangents:
        inner = jnp.mean(value * tangent, axis=-1, keepdims=True)
        outs.append((tangent * factor - value * (cube * inner)) * gain)
    return outs


def kernel(
    tokens_hbm, probes_hbm, gain_ref, wq, wk, wv, wo, qgain, kgain,
    velocity_ref, density_ref,
    W, tokens, probes, h, ext, q, o, near, away, share, dens, dens_in,
    own, stage, got,
    in_sem, stage_sem, local_sem, y_sem, send_sem, pair_sem, opp_sem, sib_sem, halo_send, halo_recv, out_sem,
):
    me = lax.axis_index("tm")
    side = lax.axis_index("segment")
    core = lax.rem(me, 2)
    x = lax.rem(me // 2, 4)
    yh = lax.rem(me // 8, 2)
    z = me // 16
    flip = core == 0

    def ring(p, d):
        return lax.rem(p + d + 4, 4)

    dev_x = [me + (ring(x, d) - x) * 2 for d in (1, -1)]
    dev_z = [me + (ring(z, d) - z) * 16 for d in (1, -1)]
    by_core = (
        jnp.where(flip, x, z),
        jnp.where(flip, z, x),
        [jnp.where(flip, i, j) for i, j in zip(dev_x, dev_z)],
        [jnp.where(flip, j, i) for i, j in zip(dev_x, dev_z)],
    )
    A, B, DEV_A, DEV_B = zip(*[by_core] * UNITS)
    sib = me + 1 - 2 * core
    far = lax.rem(me + 2 * core - 1 + 64, 64)
    dev_y = me + (1 - 2 * yh) * 8

    barrier = pltpu.get_barrier_semaphore()
    peers = [sib, dev_y, *dev_x, *dev_z, far]
    for d in peers:
        pl.semaphore_signal(barrier, inc=1, device_id={"tm": d}, device_id_type=MESH)
    pl.semaphore_signal(barrier, inc=1, device_id={"segment": 1 - side}, device_id_type=MESH)

    load_tokens = pltpu.make_async_copy(tokens_hbm, tokens, in_sem.at[0])
    load_probes = pltpu.make_async_copy(probes_hbm, probes, in_sem.at[1])
    load_tokens.start()
    load_probes.start()

    k_rows, v_rows = wk[...].astype(F32), wv[...].astype(F32)
    q_rows, o_rows = wq[...].astype(F32), wo[...].astype(F32)
    def halves(one, two):
        low = jnp.concatenate([one[:, :HALF], two[:, :HALF]], 1)
        high = jnp.concatenate([one[:, HALF:], two[:, HALF:]], 1)
        return jnp.where(flip, low, high), jnp.where(flip, high, low)

    mine_kv, theirs_kv = halves(k_rows, v_rows)
    mine_qo, theirs_qo = halves(q_rows, o_rows)
    stage[...] = jnp.concatenate([theirs_kv, theirs_qo], 0).astype(BF)
    pl.semaphore_wait(barrier, len(peers) + 1)
    swap = pltpu.make_async_remote_copy(
        src_ref=stage, dst_ref=got, send_sem=stage_sem.at[0], recv_sem=stage_sem.at[1],
        device_id={"tm": sib}, device_id_type=MESH,
    )
    swap.start()
    swap.wait()
    theirs = got[...].astype(F32)

    def both(mine, other):
        return jnp.where(
            flip, jnp.concatenate([mine, other], 0), jnp.concatenate([other, mine], 0)
        ).astype(BF)

    kv = both(mine_kv, theirs[:40])
    qo = both(mine_qo, theirs[40:])
    own[0] = kv[:, :HALF]
    own[1] = kv[:, HALF:]
    own[2] = qo[:, :HALF]
    own[3] = qo[:, HALF:]
    my_cols = pl.ds(pl.multiple_of(core * HALF, 128), HALF)
    sib_cols = pl.ds(pl.multiple_of((1 - core) * HALF, 128), HALF)

    def place(s, aa, bb):
        return jnp.where(flip, bb, aa), jnp.where(flip, aa, bb)

    def pair(s, aa, bb):
        zz, xx = place(s, aa, bb)
        return W.at[s, zz, :, xx, :, my_cols]

    def single(s, aa, y, bb):
        zz, xx = place(s, aa, bb)
        return W.at[s, zz, y, xx, :, my_cols]

    def send(ref, send_to, recv, device):
        pltpu.make_async_remote_copy(
            src_ref=ref, dst_ref=ref, send_sem=send_to, recv_sem=recv,
            device_id={"tm": device}, device_id_type=MESH,
        ).start()

    def await_ref(ref, sem):
        pltpu.make_async_copy(ref, ref, sem).wait()

    def send_pair(s, which, aa, bb):
        devs = DEV_A[s] if which == 0 else DEV_B[s]
        for k in range(2):
            send(pair(s, aa, bb), send_sem.at[s, which, k], pair_sem.at[s, aa, bb], devs[k])

    def send_single(s, which, y):
        devs = DEV_A[s] if which == 0 else DEV_B[s]
        for k in range(2):
            send(single(s, A[s], y, B[s]), send_sem.at[s, which, k], pair_sem.at[s, A[s], B[s]], devs[k])

    def send_opp(s, which, y, aa, bb):
        devs = DEV_A[s] if which == 0 else DEV_B[s]
        send(single(s, aa, y, bb), send_sem.at[s, which, y], opp_sem.at[s, y, aa, bb], devs[y])

    def to_sib(s, aa, bb):
        zz, xx = place(s, aa, bb)
        send(pair(s, aa, bb), send_sem.at[s, 2, 0], sib_sem.at[s, zz, xx], sib)

    def await_pair(s, aa, bb):
        await_ref(pair(s, aa, bb), pair_sem.at[s, aa, bb])

    def await_opp(s, aa, bb):
        for y in range(2):
            await_ref(single(s, aa, y, bb), opp_sem.at[s, y, aa, bb])

    def order(s, i):
        a = A[s]
        return jnp.where(i == 0, a, jnp.where(i == 1, ring(a, 1), jnp.where(i == 2, ring(a, -1), ring(a, 2))))

    for s in range(UNITS):
        pltpu.make_async_copy(own.at[s], single(s, A[s], yh, B[s]), local_sem.at[s]).start()
    for s in range(UNITS):
        pltpu.make_async_copy(own.at[s], single(s, A[s], yh, B[s]), local_sem.at[s]).wait()
        send(single(s, A[s], yh, B[s]), y_sem.at[s, 0], y_sem.at[s, 1], dev_y)
        send_single(s, 0, yh)
        if s == 0:
            send_single(0, 1, yh)
    load_tokens.wait()
    load_probes.wait()

    def norm_block(i):
        rows = pl.ds(pl.multiple_of(i * ROW_BLOCK, ROW_BLOCK), ROW_BLOCK)
        outs = norm_pair(
            tokens[rows].astype(F32), [probes[p, rows].astype(F32) for p in range(2)], gain_ref[...].reshape(1, WIDTH)
        )
        for p in range(3):
            h[p, rows] = outs[p].astype(BF)

    lax.fori_loop(0, ROWS // ROW_BLOCK, lambda i, c: (norm_block(i), c)[1], 0)
    part = pl.ds(pl.multiple_of(side * SEC, SEC), SEC)
    outer = pltpu.make_async_remote_copy(
        src_ref=h.at[:, pl.ds(pl.multiple_of(core * WIN, WIN), WIN), part],
        dst_ref=h.at[:, pl.ds(ROWS, WIN), part],
        send_sem=halo_send.at[2], recv_sem=halo_recv.at[2], device_id={"tm": far}, device_id_type=MESH,
    )
    relay = pltpu.make_async_remote_copy(
        src_ref=h.at[:, pl.ds(ROWS, WIN), part], dst_ref=h.at[:, pl.ds(ROWS, WIN), part],
        send_sem=halo_send.at[3], recv_sem=halo_recv.at[3], device_id={"segment": 1 - side}, device_id_type=MESH,
    )
    outer.start()

    for s in range(UNITS):
        await_ref(single(s, A[s], 1 - yh, B[s]), y_sem.at[s, 1])
        send_single(s, 0, 1 - yh)
        if s == 0:
            send_single(0, 1, 1 - yh)
        to_sib(s, A[s], B[s])
    for s in range(UNITS):
        a, b = A[s], B[s]
        await_pair(s, ring(a, -1), b)
        send_opp(s, 0, 0, ring(a, -1), b)
        await_pair(s, ring(a, 1), b)
        send_opp(s, 0, 1, ring(a, 1), b)
        if s == 0:
            send_pair(0, 1, ring(a, 1), b)
            send_pair(0, 1, ring(a, -1), b)
        to_sib(s, ring(a, 1), b)
        to_sib(s, ring(a, -1), b)
    for s in range(UNITS):
        a, b = A[s], B[s]
        await_opp(s, ring(a, 2), b)
        if s == 0:
            send_pair(0, 1, ring(a, 2), b)
        to_sib(s, ring(a, 2), b)

    def start_b(s):
        for i in range(4):
            send_pair(s, 1, order(s, i), B[s])

    def pass_b(s, i):
        aa, b = order(s, i), B[s]
        await_pair(s, aa, ring(b, -1))
        send_opp(s, 1, 0, aa, ring(b, -1))
        to_sib(s, aa, ring(b, -1))
        await_pair(s, aa, ring(b, 1))
        send_opp(s, 1, 1, aa, ring(b, 1))
        to_sib(s, aa, ring(b, 1))

    def end_b(s, i):
        aa, b = order(s, i), B[s]
        await_opp(s, aa, ring(b, 2))
        to_sib(s, aa, ring(b, 2))

    def await_sib(s):
        def body(i, _):
            zz, xx = i // 4, lax.rem(i, 4)
            await_ref(W.at[s, zz, :, xx, :, sib_cols], sib_sem.at[s, zz, xx])
            return 0

        lax.fori_loop(0, 16, body, 0)

    def first(i, _):
        pass_b(0, i)
        return 0

    lax.fori_loop(0, 4, first, 0)
    start_b(1)
    lax.fori_loop(0, 4, lambda i, c: (end_b(0, i), c)[1], 0)
    await_sib(0)

    def project(m, n, first_row, rows):
        cols = pl.ds(pl.multiple_of(n * 256, 256), 256)
        weight = W[m, :, :, :, :, cols].reshape(WIDTH, 256)
        left = h[:, first_row:first_row + rows].reshape(3 * rows, WIDTH)
        return jnp.dot(left, weight, preferred_element_type=F32).reshape(3, rows, 256)

    edge = pl.ds(pl.multiple_of(core * (ROWS + WIN), WIN), WIN)

    def to_ext(p, cols, rows):
        ext[p, pl.ds(WIN, ROWS), cols] = rows.astype(BF)

    def to_edge(p, cols, rows):
        ext[p, edge, cols] = rows.astype(BF)

    def to_q(p, cols, rows):
        q[p, :, cols] = rows.astype(BF)

    def heads_out(res, gain_ref_, n, write):
        for j in range(2):
            cols = pl.ds(pl.multiple_of(n * 256 + j * 128, 128), 128)
            part = res[:, :, j * 128:(j + 1) * 128]
            outs = norm_pair(part[0], [part[1], part[2]], gain_ref_[cols].reshape(1, 128))
            for p in range(3):
                write(p, cols, outs[p])

    def halo(base):
        return pltpu.make_async_remote_copy(
            src_ref=ext.at[pl.ds(base, 3), pl.ds(pl.multiple_of((2 - core) * WIN, WIN), WIN)],
            dst_ref=ext.at[pl.ds(base, 3), pl.ds(pl.multiple_of(core * (ROWS + WIN), WIN), WIN)],
            send_sem=halo_send.at[base // 3], recv_sem=halo_recv.at[base // 3],
            device_id={"tm": sib}, device_id_type=MESH,
        )

    def key_tile(n, _):
        heads_out(project(0, n, 0, ROWS), kgain, n, to_ext)

        @pl.when(n > 0)
        def _():
            pass_b(1, n - 1)

        return 0

    outer.wait()
    relay.start()
    lax.fori_loop(0, 5, key_tile, 0)
    halo(0).start()
    start_b(2)
    lax.fori_loop(0, 4, lambda i, c: (end_b(1, i), c)[1], 0)
    await_sib(1)

    def value_tile(n, _):
        @pl.when(n > 0)
        def _():
            pass_b(2, n - 1)

        res = project(1, n, 0, ROWS)
        cols = pl.ds(pl.multiple_of(n * 256, 256), 256)
        for p in range(3):
            to_ext(3 + p, cols, res[p])
        return 0

    lax.fori_loop(0, 5, value_tile, 0)
    start_b(3)
    halo(3).start()

    def edge_tile(n, _):
        heads_out(project(0, n, ROWS, WIN), kgain, n, to_edge)
        res = project(1, n, ROWS, WIN)
        cols = pl.ds(pl.multiple_of(n * 256, 256), 256)
        for p in range(3):
            to_edge(3 + p, cols, res[p])
        return 0

    relay.wait()
    lax.fori_loop(0, 5, edge_tile, 0)
    lax.fori_loop(0, 4, lambda i, c: (end_b(2, i), c)[1], 0)
    await_sib(2)

    def query_tile(n, _):
        @pl.when(n < 4)
        def _():
            pass_b(3, n)

        heads_out(project(2, n, 0, ROWS), qgain, n, to_q)
        return 0

    lax.fori_loop(0, 5, query_tile, 0)
    halo(0).wait()
    halo(3).wait()

    scale = 1.0 / math.sqrt(HEAD)
    u = lax.broadcasted_iota(jnp.int32, (WIN, 3 * WIN), 0)
    w = lax.broadcasted_iota(jnp.int32, (WIN, 3 * WIN), 1)
    band = (w - u >= 0) & (w - u <= 2 * WIN)
    NT = (((1,), (1,)), ((), ()))

    def attend(head, block):
        cols = pl.ds(pl.multiple_of(head * HEAD, HEAD), HEAD)
        rows = pl.ds(pl.multiple_of(block * WIN, WIN), WIN)
        keys = pl.ds(pl.multiple_of(block * WIN, WIN), 3 * WIN)
        place_ = me * ROWS - WIN + block * WIN + w
        valid = band & (place_ >= 0) & (place_ < 64 * ROWS)
        qn, dq0, dq1 = [q[p, rows, cols] for p in range(3)]
        k, dk0, dk1, v, dv0, dv1 = [ext[p, keys, cols] for p in range(6)]
        zero = jnp.zeros_like(qn)
        left = jnp.concatenate(
            [jnp.concatenate([qn, zero], 1), jnp.concatenate([dq0, qn], 1)], 0
        )
        first_ = lax.dot_general(left, jnp.concatenate([k, dk0], 1), NT, preferred_element_type=F32)
        second = lax.dot_general(
            jnp.concatenate([dq1, qn], 1), jnp.concatenate([k, dk1], 1), NT, preferred_element_type=F32
        )
        e = jnp.where(valid, jnp.exp(first_[:WIN] * scale), 0.0)
        weights = e * (1.0 / jnp.sum(e, axis=-1, keepdims=True))
        tans = []
        for ds in (first_[WIN:], second):
            ds = jnp.where(valid, ds * scale, 0.0)
            tans.append(weights * (ds - jnp.sum(weights * ds, axis=-1, keepdims=True)))
        low = weights.astype(BF)
        stack = jnp.concatenate([low, tans[0].astype(BF), tans[1].astype(BF)], 0)
        by_v = jnp.dot(stack, v, preferred_element_type=F32)
        by_dv = jnp.dot(low, jnp.concatenate([dv0, dv1], 1), preferred_element_type=F32)
        o[0, rows, cols] = by_v[:WIN].astype(BF)
        o[1, rows, cols] = (by_v[WIN:2 * WIN] + by_dv[:, :HEAD]).astype(BF)
        o[2, rows, cols] = (by_v[2 * WIN:] + by_dv[:, HEAD:]).astype(BF)

    def give(block):
        return pltpu.make_async_remote_copy(
            src_ref=away.at[block], dst_ref=share.at[block],
            send_sem=out_sem.at[block, 0], recv_sem=out_sem.at[block, 1],
            device_id={"segment": 1 - side}, device_id_type=MESH,
        )

    def out_half(left, half):
        weight = W[3, pl.ds(2 * half, 2)].reshape(SEC, SEC)
        return lax.dot_general(left, weight, NT, preferred_element_type=F32)

    def block_step(block, _):
        lax.fori_loop(0, HEADS // 2, lambda i, c: (attend(2 * i, block), attend(2 * i + 1, block), c)[2], 0)

        @pl.when(block == 0)
        def _():
            lax.fori_loop(0, 4, lambda i, c: (end_b(3, i), c)[1], 0)
            await_sib(3)

        rows = pl.ds(pl.multiple_of(block * WIN, WIN), WIN)
        away[block] = out_half(o[0, rows], 1 - side).astype(BF)
        give(block).start()
        return 0

    lax.fori_loop(0, 2, block_step, 0)
    near[...] = out_half(o[0], side)
    dens[...] = jnp.zeros_like(dens)

    def trace_step(i, _):
        p, half = i // 2, lax.rem(i, 2)
        dy = out_half(o[1 + p], half)
        prod = dy * probes[p, :, pl.ds(pl.multiple_of(half * SEC, SEC), SEC)].astype(F32)
        total = prod[:, :128]
        for j in range(1, SEC // 128):
            total = total + prod[:, j * 128:(j + 1) * 128]
        dens[...] += jnp.sum(total.T, axis=0, keepdims=True)
        return 0

    lax.fori_loop(0, 4, trace_step, 0)
    give_dens = pltpu.make_async_remote_copy(
        src_ref=dens, dst_ref=dens_in, send_sem=out_sem.at[2, 0], recv_sem=out_sem.at[2, 1],
        device_id={"segment": 1 - side}, device_id_type=MESH,
    )
    give_dens.start()
    for block in range(2):
        give(block).wait()
        rows = pl.ds(block * WIN, WIN)
        velocity_ref[rows] = (near[rows] + share[block].astype(F32)).astype(BF)
    give_dens.wait()
    density_ref[...] = (dens[0] + dens_in[0]) * (1.0 / (2 * math.sqrt(WIDTH)))

    for s in range(UNITS):
        await_ref(single(s, A[s], yh, B[s]), y_sem.at[s, 0])
        for k in range(2):
            for which in range(2):
                n = 3 if which == 0 else 12
                ref = W.at[0].at[pl.ds(0, 1), 0, pl.ds(0, 3)] if n == 3 else W.at[0].at[:, 0, pl.ds(0, 3)]
                ref = ref.at[:, :, :, my_cols]
                await_ref(ref, send_sem.at[s, which, k])
        await_ref(W.at[0].at[:, :, :, :, my_cols], send_sem.at[s, 2, 0])


def layer(tokens, probes, norm_gain, w_query, w_key, w_value, query_gain, key_gain, w_out):
    vmem = pl.BlockSpec(memory_space=pltpu.VMEM)
    hbm = pl.BlockSpec(memory_space=pl.ANY)
    V, D, R = pltpu.VMEM, pltpu.SemaphoreType.DMA, None
    velocity, density = pl.pallas_call(
        kernel,
        out_shape=(
            jax.ShapeDtypeStruct((ROWS, SEC), BF),
            jax.ShapeDtypeStruct((ROWS,), F32),
        ),
        in_specs=[hbm, hbm] + [vmem] * 7,
        out_specs=(vmem, vmem),
        scratch_shapes=[
            V((4, 4, 2, 4, PIECE, SEC), BF),
            V((ROWS, WIDTH), BF),
            V((2, ROWS, WIDTH), jnp.int32),
            V((3, ROWS + WIN, WIDTH), BF),
            V((6, ROWS + 2 * WIN, SEC), BF),
            V((3, ROWS, SEC), BF),
            V((3, ROWS, SEC), BF),
            V((ROWS, SEC), F32),
            V((2, WIN, SEC), BF),
            V((2, WIN, SEC), BF),
            V((8, ROWS), F32),
            V((8, ROWS), F32),
            V((UNITS, PIECE, HALF), BF),
            V((PIECE, SEC), BF),
            V((PIECE, SEC), BF),
            D((2,)), D((2,)), D((UNITS,)), D((UNITS, 2)), D((UNITS, 3, 2)),
            D((UNITS, 4, 4)), D((UNITS, 2, 4, 4)), D((UNITS, 4, 4)),
            D((4,)), D((4,)), D((3, 2)),
        ],
        compiler_params=pltpu.CompilerParams(
            collective_id=0, has_side_effects=True, vmem_limit_bytes=60 * 2**20
        ),
    )(
        tokens, probes, norm_gain, w_query, w_key, w_value, w_out,
        query_gain, key_gain,
    )
    return velocity, density


def solution(mesh):
    placed = (
        P("tm", None),
        P(None, "tm", None),
        P(),
        P("tm", "segment"),
        P("tm", "segment"),
        P("tm", "segment"),
        P("segment"),
        P("segment"),
        P("tm", "segment"),
    )
    return jax.shard_map(
        layer, mesh=mesh, in_specs=placed, out_specs=(P("tm", "segment"), P("tm")), check_vma=False
    )
```

```python
import math

import jax
import jax.numpy as jnp
from jax import lax
from jax.experimental import pallas as pl
from jax.experimental.pallas import tpu as pltpu
from jax.sharding import PartitionSpec as P

MESH = pl.DeviceIdType.MESH
HEAD = 128
WIN = 128
EPS = 1e-06
BF = jnp.bfloat16
F32 = jnp.float32

ROWS = 256
WIDTH = 2560
SEC = 1280
HALF = 640
PIECE = 80
HEADS = 10
ROW_BLOCK = 16

UNITS = 4


def norm_pair(value, tangents, gain):
    factor = lax.rsqrt(jnp.mean(value * value, axis=-1, keepdims=True) + EPS)
    cube = factor * factor * factor
    outs = [value * factor * gain]
    for tangent in tangents:
        inner = jnp.mean(value * tangent, axis=-1, keepdims=True)
        outs.append((tangent * factor - value * (cube * inner)) * gain)
    return outs


def kernel(
    tokens_hbm, probes_hbm, gain_ref, wq, wk, wv, wo, qgain, kgain,
    velocity_ref, density_ref,
    W, tokens, probes, h, ext, q, o, near, away, share, dens, dens_in,
    own, stage, got,
    in_sem, stage_sem, local_sem, y_sem, send_sem, pair_sem, opp_sem, sib_sem, halo_send, halo_recv, out_sem,
):
    me = lax.axis_index("tm")
    side = lax.axis_index("segment")
    core = lax.rem(me, 2)
    x = lax.rem(me // 2, 4)
    yh = lax.rem(me // 8, 2)
    z = me // 16
    flip = core == 0

    def ring(p, d):
        return lax.rem(p + d + 4, 4)

    dev_x = [me + (ring(x, d) - x) * 2 for d in (1, -1)]
    dev_z = [me + (ring(z, d) - z) * 16 for d in (1, -1)]
    by_core = (
        jnp.where(flip, x, z),
        jnp.where(flip, z, x),
        [jnp.where(flip, i, j) for i, j in zip(dev_x, dev_z)],
        [jnp.where(flip, j, i) for i, j in zip(dev_x, dev_z)],
    )
    A, B, DEV_A, DEV_B = zip(*[by_core] * UNITS)
    sib = me + 1 - 2 * core
    far = lax.rem(me + 2 * core - 1 + 64, 64)
    dev_y = me + (1 - 2 * yh) * 8

    barrier = pltpu.get_barrier_semaphore()
    peers = [sib, dev_y, *dev_x, *dev_z, far]
    for d in peers:
        pl.semaphore_signal(barrier, inc=1, device_id={"tm": d}, device_id_type=MESH)
    pl.semaphore_signal(barrier, inc=1, device_id={"segment": 1 - side}, device_id_type=MESH)

    load_tokens = pltpu.make_async_copy(tokens_hbm, tokens, in_sem.at[0])
    load_probes = pltpu.make_async_copy(probes_hbm, probes, in_sem.at[1])
    load_tokens.start()
    load_probes.start()

    k_rows, v_rows = wk[...].astype(F32), wv[...].astype(F32)
    q_rows, o_rows = wq[...].astype(F32), wo[...].astype(F32)
    def halves(one, two):
        low = jnp.concatenate([one[:, :HALF], two[:, :HALF]], 1)
        high = jnp.concatenate([one[:, HALF:], two[:, HALF:]], 1)
        return jnp.where(flip, low, high), jnp.where(flip, high, low)

    mine_kv, theirs_kv = halves(k_rows, v_rows)
    mine_qo, theirs_qo = halves(q_rows, o_rows)
    stage[...] = jnp.concatenate([theirs_kv, theirs_qo], 0).astype(BF)
    pl.semaphore_wait(barrier, len(peers) + 1)
    swap = pltpu.make_async_remote_copy(
        src_ref=stage, dst_ref=got, send_sem=stage_sem.at[0], recv_sem=stage_sem.at[1],
        device_id={"tm": sib}, device_id_type=MESH,
    )
    swap.start()
    swap.wait()
    theirs = got[...].astype(F32)

    def both(mine, other):
        return jnp.where(
            flip, jnp.concatenate([mine, other], 0), jnp.concatenate([other, mine], 0)
        ).astype(BF)

    kv = both(mine_kv, theirs[:40])
    qo = both(mine_qo, theirs[40:])
    own[0] = kv[:, :HALF]
    own[1] = kv[:, HALF:]
    own[2] = qo[:, :HALF]
    own[3] = qo[:, HALF:]
    my_cols = pl.ds(pl.multiple_of(core * HALF, 128), HALF)
    sib_cols = pl.ds(pl.multiple_of((1 - core) * HALF, 128), HALF)

    def place(s, aa, bb):
        return jnp.where(flip, bb, aa), jnp.where(flip, aa, bb)

    def pair(s, aa, bb):
        zz, xx = place(s, aa, bb)
        return W.at[s, zz, :, xx, :, my_cols]

    def single(s, aa, y, bb):
        zz, xx = place(s, aa, bb)
        return W.at[s, zz, y, xx, :, my_cols]

    def send(ref, send_to, recv, device):
        pltpu.make_async_remote_copy(
            src_ref=ref, dst_ref=ref, send_sem=send_to, recv_sem=recv,
            device_id={"tm": device}, device_id_type=MESH,
        ).start()

    def await_ref(ref, sem):
        pltpu.make_async_copy(ref, ref, sem).wait()

    def send_pair(s, which, aa, bb):
        devs = DEV_A[s] if which == 0 else DEV_B[s]
        for k in range(2):
            send(pair(s, aa, bb), send_sem.at[s, which, k], pair_sem.at[s, aa, bb], devs[k])

    def send_single(s, which, y):
        devs = DEV_A[s] if which == 0 else DEV_B[s]
        for k in range(2):
            send(single(s, A[s], y, B[s]), send_sem.at[s, which, k], pair_sem.at[s, A[s], B[s]], devs[k])

    def send_opp(s, which, y, aa, bb):
        devs = DEV_A[s] if which == 0 else DEV_B[s]
        send(single(s, aa, y, bb), send_sem.at[s, which, y], opp_sem.at[s, y, aa, bb], devs[y])

    def to_sib(s, aa, bb):
        zz, xx = place(s, aa, bb)
        send(pair(s, aa, bb), send_sem.at[s, 2, 0], sib_sem.at[s, zz, xx], sib)

    def await_pair(s, aa, bb):
        await_ref(pair(s, aa, bb), pair_sem.at[s, aa, bb])

    def await_opp(s, aa, bb):
        for y in range(2):
            await_ref(single(s, aa, y, bb), opp_sem.at[s, y, aa, bb])

    def order(s, i):
        a = A[s]
        return jnp.where(i == 0, a, jnp.where(i == 1, ring(a, 1), jnp.where(i == 2, ring(a, -1), ring(a, 2))))

    for s in range(UNITS):
        pltpu.make_async_copy(own.at[s], single(s, A[s], yh, B[s]), local_sem.at[s]).start()
    for s in range(UNITS):
        pltpu.make_async_copy(own.at[s], single(s, A[s], yh, B[s]), local_sem.at[s]).wait()
        send(single(s, A[s], yh, B[s]), y_sem.at[s, 0], y_sem.at[s, 1], dev_y)
        send_single(s, 0, yh)
        if s == 0:
            send_single(0, 1, yh)
    load_tokens.wait()
    load_probes.wait()

    def norm_block(i):
        rows = pl.ds(pl.multiple_of(i * ROW_BLOCK, ROW_BLOCK), ROW_BLOCK)
        outs = norm_pair(
            tokens[rows].astype(F32), [probes[p, rows].astype(F32) for p in range(2)], gain_ref[...].reshape(1, WIDTH)
        )
        for p in range(3):
            h[p, rows] = outs[p].astype(BF)

    lax.fori_loop(0, ROWS // ROW_BLOCK, lambda i, c: (norm_block(i), c)[1], 0)
    part = pl.ds(pl.multiple_of(side * SEC, SEC), SEC)
    outer = pltpu.make_async_remote_copy(
        src_ref=h.at[:, pl.ds(pl.multiple_of(core * WIN, WIN), WIN), part],
        dst_ref=h.at[:, pl.ds(ROWS, WIN), part],
        send_sem=halo_send.at[2], recv_sem=halo_recv.at[2], device_id={"tm": far}, device_id_type=MESH,
    )
    relay = pltpu.make_async_remote_copy(
        src_ref=h.at[:, pl.ds(ROWS, WIN), part], dst_ref=h.at[:, pl.ds(ROWS, WIN), part],
        send_sem=halo_send.at[3], recv_sem=halo_recv.at[3], device_id={"segment": 1 - side}, device_id_type=MESH,
    )
    outer.start()

    for s in range(UNITS):
        await_ref(single(s, A[s], 1 - yh, B[s]), y_sem.at[s, 1])
        send_single(s, 0, 1 - yh)
        if s == 0:
            send_single(0, 1, 1 - yh)
        to_sib(s, A[s], B[s])
    for s in range(UNITS):
        a, b = A[s], B[s]
        await_pair(s, ring(a, -1), b)
        send_opp(s, 0, 0, ring(a, -1), b)
        await_pair(s, ring(a, 1), b)
        send_opp(s, 0, 1, ring(a, 1), b)
        if s == 0:
            send_pair(0, 1, ring(a, 1), b)
            send_pair(0, 1, ring(a, -1), b)
        to_sib(s, ring(a, 1), b)
        to_sib(s, ring(a, -1), b)
    for s in range(UNITS):
        a, b = A[s], B[s]
        await_opp(s, ring(a, 2), b)
        if s == 0:
            send_pair(0, 1, ring(a, 2), b)
        to_sib(s, ring(a, 2), b)

    def start_b(s):
        for i in range(4):
            send_pair(s, 1, order(s, i), B[s])

    def pass_b(s, i):
        aa, b = order(s, i), B[s]
        await_pair(s, aa, ring(b, -1))
        send_opp(s, 1, 0, aa, ring(b, -1))
        to_sib(s, aa, ring(b, -1))
        await_pair(s, aa, ring(b, 1))
        send_opp(s, 1, 1, aa, ring(b, 1))
        to_sib(s, aa, ring(b, 1))

    def end_b(s, i):
        aa, b = order(s, i), B[s]
        await_opp(s, aa, ring(b, 2))
        to_sib(s, aa, ring(b, 2))

    def await_sib(s):
        def body(i, _):
            zz, xx = i // 4, lax.rem(i, 4)
            await_ref(W.at[s, zz, :, xx, :, sib_cols], sib_sem.at[s, zz, xx])
            return 0

        lax.fori_loop(0, 16, body, 0)

    def first(i, _):
        pass_b(0, i)
        return 0

    lax.fori_loop(0, 4, first, 0)
    start_b(1)
    lax.fori_loop(0, 4, lambda i, c: (end_b(0, i), c)[1], 0)
    await_sib(0)

    def project(m, n, first_row, rows):
        cols = pl.ds(pl.multiple_of(n * 256, 256), 256)
        weight = W[m, :, :, :, :, cols].reshape(WIDTH, 256)
        left = h[:, first_row:first_row + rows].reshape(3 * rows, WIDTH)
        return jnp.dot(left, weight, preferred_element_type=F32).reshape(3, rows, 256)

    edge = pl.ds(pl.multiple_of(core * (ROWS + WIN), WIN), WIN)

    def to_ext(p, cols, rows):
        ext[p, pl.ds(WIN, ROWS), cols] = rows.astype(BF)

    def to_edge(p, cols, rows):
        ext[p, edge, cols] = rows.astype(BF)

    def to_q(p, cols, rows):
        q[p, :, cols] = rows.astype(BF)

    def heads_out(res, gain_ref_, n, write):
        for j in range(2):
            cols = pl.ds(pl.multiple_of(n * 256 + j * 128, 128), 128)
            part = res[:, :, j * 128:(j + 1) * 128]
            outs = norm_pair(part[0], [part[1], part[2]], gain_ref_[cols].reshape(1, 128))
            for p in range(3):
                write(p, cols, outs[p])

    def halo(base):
        return pltpu.make_async_remote_copy(
            src_ref=ext.at[pl.ds(base, 3), pl.ds(pl.multiple_of((2 - core) * WIN, WIN), WIN)],
            dst_ref=ext.at[pl.ds(base, 3), pl.ds(pl.multiple_of(core * (ROWS + WIN), WIN), WIN)],
            send_sem=halo_send.at[base // 3], recv_sem=halo_recv.at[base // 3],
            device_id={"tm": sib}, device_id_type=MESH,
        )

    def key_tile(n, _):
        heads_out(project(0, n, 0, ROWS), kgain, n, to_ext)

        @pl.when(n > 0)
        def _():
            pass_b(1, n - 1)

        return 0

    outer.wait()
    relay.start()
    lax.fori_loop(0, 5, key_tile, 0)
    halo(0).start()
    start_b(2)
    lax.fori_loop(0, 4, lambda i, c: (end_b(1, i), c)[1], 0)
    await_sib(1)

    def value_tile(n, _):
        @pl.when(n > 0)
        def _():
            pass_b(2, n - 1)

        res = project(1, n, 0, ROWS)
        cols = pl.ds(pl.multiple_of(n * 256, 256), 256)
        for p in range(3):
            to_ext(3 + p, cols, res[p])
        return 0

    lax.fori_loop(0, 5, value_tile, 0)
    start_b(3)
    halo(3).start()

    def edge_tile(n, _):
        heads_out(project(0, n, ROWS, WIN), kgain, n, to_edge)
        res = project(1, n, ROWS, WIN)
        cols = pl.ds(pl.multiple_of(n * 256, 256), 256)
        for p in range(3):
            to_edge(3 + p, cols, res[p])
        return 0

    relay.wait()
    lax.fori_loop(0, 5, edge_tile, 0)
    lax.fori_loop(0, 4, lambda i, c: (end_b(2, i), c)[1], 0)
    await_sib(2)

    def query_tile(n, _):
        @pl.when(n < 4)
        def _():
            pass_b(3, n)

        heads_out(project(2, n, 0, ROWS), qgain, n, to_q)
        return 0

    lax.fori_loop(0, 5, query_tile, 0)
    halo(0).wait()
    halo(3).wait()

    scale = 1.0 / math.sqrt(HEAD)
    u = lax.broadcasted_iota(jnp.int32, (WIN, 3 * WIN), 0)
    w = lax.broadcasted_iota(jnp.int32, (WIN, 3 * WIN), 1)
    band = (w - u >= 0) & (w - u <= 2 * WIN)
    NT = (((1,), (1,)), ((), ()))

    def attend(head, block):
        cols = pl.ds(pl.multiple_of(head * HEAD, HEAD), HEAD)
        rows = pl.ds(pl.multiple_of(block * WIN, WIN), WIN)
        keys = pl.ds(pl.multiple_of(block * WIN, WIN), 3 * WIN)
        place_ = me * ROWS - WIN + block * WIN + w
        valid = band & (place_ >= 0) & (place_ < 64 * ROWS)
        qn, dq0, dq1 = [q[p, rows, cols] for p in range(3)]
        k, dk0, dk1, v, dv0, dv1 = [ext[p, keys, cols] for p in range(6)]
        zero = jnp.zeros_like(qn)
        left = jnp.concatenate(
            [jnp.concatenate([qn, zero], 1), jnp.concatenate([dq0, qn], 1)], 0
        )
        first_ = lax.dot_general(left, jnp.concatenate([k, dk0], 1), NT, preferred_element_type=F32)
        second = lax.dot_general(
            jnp.concatenate([dq1, qn], 1), jnp.concatenate([k, dk1], 1), NT, preferred_element_type=F32
        )
        e = jnp.where(valid, jnp.exp(first_[:WIN] * scale), 0.0)
        weights = e * (1.0 / jnp.sum(e, axis=-1, keepdims=True))
        tans = []
        for ds in (first_[WIN:], second):
            ds = jnp.where(valid, ds * scale, 0.0)
            tans.append(weights * (ds - jnp.sum(weights * ds, axis=-1, keepdims=True)))
        low = weights.astype(BF)
        stack = jnp.concatenate([low, tans[0].astype(BF), tans[1].astype(BF)], 0)
        by_v = jnp.dot(stack, v, preferred_element_type=F32)
        by_dv = jnp.dot(low, jnp.concatenate([dv0, dv1], 1), preferred_element_type=F32)
        o[0, rows, cols] = by_v[:WIN].astype(BF)
        o[1, rows, cols] = (by_v[WIN:2 * WIN] + by_dv[:, :HEAD]).astype(BF)
        o[2, rows, cols] = (by_v[2 * WIN:] + by_dv[:, HEAD:]).astype(BF)

    def give(block):
        return pltpu.make_async_remote_copy(
            src_ref=away.at[block], dst_ref=share.at[block],
            send_sem=out_sem.at[block, 0], recv_sem=out_sem.at[block, 1],
            device_id={"segment": 1 - side}, device_id_type=MESH,
        )

    def out_half(left, half):
        weight = W[3, pl.ds(2 * half, 2)].reshape(SEC, SEC)
        return lax.dot_general(left, weight, NT, preferred_element_type=F32)

    def block_step(block, _):
        lax.fori_loop(0, 2, lambda i, c: ([attend(5 * i + k, block) for k in range(5)], c)[1], 0)

        @pl.when(block == 0)
        def _():
            lax.fori_loop(0, 4, lambda i, c: (end_b(3, i), c)[1], 0)
            await_sib(3)

        rows = pl.ds(pl.multiple_of(block * WIN, WIN), WIN)
        away[block] = out_half(o[0, rows], 1 - side).astype(BF)
        give(block).start()
        return 0

    lax.fori_loop(0, 2, block_step, 0)
    near[...] = out_half(o[0], side)
    dens[...] = jnp.zeros_like(dens)

    def trace_step(i, _):
        p, half = i // 2, lax.rem(i, 2)
        dy = out_half(o[1 + p], half)
        prod = dy * probes[p, :, pl.ds(pl.multiple_of(half * SEC, SEC), SEC)].astype(F32)
        total = prod[:, :128]
        for j in range(1, SEC // 128):
            total = total + prod[:, j * 128:(j + 1) * 128]
        dens[...] += jnp.sum(total.T, axis=0, keepdims=True)
        return 0

    lax.fori_loop(0, 4, trace_step, 0)
    give_dens = pltpu.make_async_remote_copy(
        src_ref=dens, dst_ref=dens_in, send_sem=out_sem.at[2, 0], recv_sem=out_sem.at[2, 1],
        device_id={"segment": 1 - side}, device_id_type=MESH,
    )
    give_dens.start()
    for block in range(2):
        give(block).wait()
        rows = pl.ds(block * WIN, WIN)
        velocity_ref[rows] = (near[rows] + share[block].astype(F32)).astype(BF)
    give_dens.wait()
    density_ref[...] = (dens[0] + dens_in[0]) * (1.0 / (2 * math.sqrt(WIDTH)))

    for s in range(UNITS):
        await_ref(single(s, A[s], yh, B[s]), y_sem.at[s, 0])
        for k in range(2):
            for which in range(2):
                n = 3 if which == 0 else 12
                ref = W.at[0].at[pl.ds(0, 1), 0, pl.ds(0, 3)] if n == 3 else W.at[0].at[:, 0, pl.ds(0, 3)]
                ref = ref.at[:, :, :, my_cols]
                await_ref(ref, send_sem.at[s, which, k])
        await_ref(W.at[0].at[:, :, :, :, my_cols], send_sem.at[s, 2, 0])


def layer(tokens, probes, norm_gain, w_query, w_key, w_value, query_gain, key_gain, w_out):
    vmem = pl.BlockSpec(memory_space=pltpu.VMEM)
    hbm = pl.BlockSpec(memory_space=pl.ANY)
    V, D, R = pltpu.VMEM, pltpu.SemaphoreType.DMA, None
    velocity, density = pl.pallas_call(
        kernel,
        out_shape=(
            jax.ShapeDtypeStruct((ROWS, SEC), BF),
            jax.ShapeDtypeStruct((ROWS,), F32),
        ),
        in_specs=[hbm, hbm] + [vmem] * 7,
        out_specs=(vmem, vmem),
        scratch_shapes=[
            V((4, 4, 2, 4, PIECE, SEC), BF),
            V((ROWS, WIDTH), BF),
            V((2, ROWS, WIDTH), jnp.int32),
            V((3, ROWS + WIN, WIDTH), BF),
            V((6, ROWS + 2 * WIN, SEC), BF),
            V((3, ROWS, SEC), BF),
            V((3, ROWS, SEC), BF),
            V((ROWS, SEC), F32),
            V((2, WIN, SEC), BF),
            V((2, WIN, SEC), BF),
            V((8, ROWS), F32),
            V((8, ROWS), F32),
            V((UNITS, PIECE, HALF), BF),
            V((PIECE, SEC), BF),
            V((PIECE, SEC), BF),
            D((2,)), D((2,)), D((UNITS,)), D((UNITS, 2)), D((UNITS, 3, 2)),
            D((UNITS, 4, 4)), D((UNITS, 2, 4, 4)), D((UNITS, 4, 4)),
            D((4,)), D((4,)), D((3, 2)),
        ],
        compiler_params=pltpu.CompilerParams(
            collective_id=0, has_side_effects=True, vmem_limit_bytes=60 * 2**20
        ),
    )(
        tokens, probes, norm_gain, w_query, w_key, w_value, w_out,
        query_gain, key_gain,
    )
    return velocity, density


def solution(mesh):
    placed = (
        P("tm", None),
        P(None, "tm", None),
        P(),
        P("tm", "segment"),
        P("tm", "segment"),
        P("tm", "segment"),
        P("segment"),
        P("segment"),
        P("tm", "segment"),
    )
    return jax.shard_map(
        layer, mesh=mesh, in_specs=placed, out_specs=(P("tm", "segment"), P("tm")), check_vma=False
    )
```
